1024 devices in a mesh: shard: 64 (over y, x, core), rep: 16 (over z).
Axes of the slice: x: 4, y: 8, z: 16, core: 2. Of those that a mesh axis runs over, the one named last changes fastest.
Arguments:
- table_a: bfloat16 [65536, 64], P('shard'), may hold values from -6 to 6
- table_b: bfloat16 [65536, 32], P('shard'), may hold values from -6 to 6
- proj_a: bfloat16 [64, 256], replicated, may hold values from -0.75 to 0.75
- proj_b: bfloat16 [32, 256], replicated, may hold values from -1 to 1
- owner_a: int32 [1048576, 1], P(('shard', 'rep')), may hold values from 0 to 63; in each aligned block of 1024 rows (0 to 1023, 1024 to 2047, ...) at most 24 rows name the same one
- row_a: int32 [1048576], P(('shard', 'rep')), may hold values from 0 to 1023
- bag_a: int32 [1024, 1024], P(('shard', 'rep')), may hold values from 0 to 511, never falling along the last dimension, each value on 1 to 4 neighbouring positions
- owner_b: int32 [1048576, 1], P(('shard', 'rep')), may hold values from 0 to 63; in each aligned block of 1024 rows (0 to 1023, 1024 to 2047, ...) at most 24 rows name the same one
- row_b: int32 [1048576], P(('shard', 'rep')), may hold values from 0 to 1023
- bag_b: int32 [1024, 1024], P(('shard', 'rep')), may hold values from 0 to 511, never falling along the last dimension, each value on 1 to 4 neighbouring positions
- d_pooled: bfloat16 [524288, 256], P(('shard', 'rep')), may hold values from -6 to 6
Outputs:
- pooled: bfloat16 [524288, 256], P(('shard', 'rep'))
- grad_table_a: float32 [65536, 64], P('shard')
- grad_table_b: float32 [65536, 32], P('shard')
- grad_proj_a: float32 [64, 256], replicated
- grad_proj_b: float32 [32, 256], replicated
The draws below stay inside these ranges and needn't reach their ends.
Inputs may be any that keep to these rules, and one draw needn't show every extreme that they name: `owner_a`: among the lookups of one device, at most 24 name the same owner; some owner is named by exactly 24. `owner_b`: among the lookups of one device, at most 24 name the same owner; some owner is named by exactly 24. `bag_a`: along each device's row the bag never falls; every bag has 1 to 4 lookups, some exactly 4. `bag_b`: along each device's row the bag never falls; every bag has 1 to 4 lookups, some exactly 4.
All inputs are finite; a program needn't handle non-finite values.
Results may differ from the reference program's by a relative error of at most 0.0065.
Values may be sent and summed in bfloat16 or wider, within the bound.
A program may use at most 32 MiB of HBM per device.

```python
import math
import jax
import jax.numpy as jnp
import numpy as np

W_A = 64
W_B = 32
E = 256
ROWS_DEV = 1024
BAGS = 512
LOOK = 1024
CAP = 24
ROWS_A = 65536
ROWS_B = 65536
BAGS_ALL = 524288
LOOK_ALL = 1048576
N_SHARD = 64
N_REP = 16


def place_ends(drawn, key, smallest, high):
    index_at = [jax.random.randint(jax.random.fold_in(key, axis), (), 0, length) for axis, length in enumerate(drawn.shape)]
    widest = drawn.shape.index(max(drawn.shape))
    beside = index_at[:widest] + [(index_at[widest] + 1) % drawn.shape[widest]] + index_at[widest + 1:]
    return drawn.at[tuple(index_at)].set(smallest).at[tuple(beside)].set(high)


def block_levels(rng, shape, cuts, smallest, high):
    factor_of, own = 1.0, jax.random.fold_in(rng, 6)
    for position, shards_of in cuts:
        heights = jnp.exp(jax.random.uniform(jax.random.fold_in(own, position), (shards_of,), jnp.float32, smallest / len(cuts), high / len(cuts)))
        factor_of = factor_of * jnp.repeat(heights, shape[position] // shards_of).reshape([-1 if axis == position else 1 for axis in range(len(shape))])
    return factor_of


def split_up(amount, total, most, slope):
    weights = [(1 << 20) // math.isqrt(standing ** slope) + 1 for standing in range(2, amount + 1)]
    surplus, holding = total - most - (amount - 1), [1] * (amount - 1)
    while surplus > 0:
        movable = [i for i in range(amount - 1) if holding[i] < most]
        whole, budget = sum([weights[i] for i in movable]), surplus
        for i in movable:
            extra = min(most - holding[i], max(1, budget * weights[i] // whole), surplus)
            holding[i] = holding[i] + extra
            surplus = surplus - extra
    return np.array([most] + holding)


def uneven_parts(key, amount, total, bound, skew):
    if amount == 2:
        one = jax.random.randint(key, (), max(1, total - bound), min(bound, total - 1) + 1)
        return jnp.stack([one, total - one])
    lengths = jnp.asarray(split_up(amount, total, bound, skew), jnp.int32)
    pairs = (amount - 1) // 2
    donor, sink = lengths[1:1 + 2 * pairs:2], lengths[2:2 + 2 * pairs:2]
    slack = jnp.minimum(donor - 1, bound - sink)
    moved = jax.random.randint(jax.random.fold_in(key, 1), (pairs,), 0, 1 << 20) % (slack + 1)
    lengths = lengths.at[1:1 + 2 * pairs:2].set(donor - moved).at[2:2 + 2 * pairs:2].set(sink + moved)
    return lengths[jax.random.permutation(jax.random.fold_in(key, 2), amount)]


def assign_block(rng, own, number, rows, amount, top, limit, slope):
    order = jax.random.permutation(rng, amount)
    packed, common = shares(amount, rows * top, limit, slope, True), shares(amount, rows * top, limit, slope, False)
    places = jnp.arange(amount)

    def named(tallies, turn):
        used = int((tallies > 0).sum())
        fixed = max(1, used // 4)
        passed = fixed + (places - fixed + turn * (used - fixed)) % max(1, amount - fixed)
        return jnp.zeros((amount,), jnp.int32).at[order[jnp.where(places < fixed, places, passed)]].set(jnp.asarray(tallies, jnp.int32))

    tallies = jnp.where(number % 4 == 0, named(packed, number // 4), named(common, number - number // 4 - 1))
    mixed = jax.random.permutation(jax.random.fold_in(own, 3), amount)
    donor, sink = mixed[0:amount // 2 * 2:2], mixed[1:amount // 2 * 2:2]
    margin = jnp.minimum(tallies[donor] - 1, limit - tallies[sink]) // 2
    margin = jnp.where((donor == order[0]) | (sink == order[0]) | (tallies[sink] == 0), 0, jnp.maximum(margin, 0))
    passed = jax.random.randint(jax.random.fold_in(own, 4), (amount // 2,), 0, 1 << 20) % (margin + 1)
    tallies = tallies.at[donor].add(-passed).at[sink].add(passed)
    members = jnp.searchsorted(jnp.cumsum(tallies), jnp.arange(rows * top), side="right").astype(jnp.int32)
    listing = members.reshape(top, rows).T
    listing = listing[jax.random.permutation(jax.random.fold_in(own, 1), rows)]
    turn = jax.random.randint(jax.random.fold_in(own, 2), (rows, 1), 0, top)
    return jnp.take_along_axis(listing, (jnp.arange(top)[None, :] + turn) % top, axis=1)


def shares(amount, total, bound, lean, full):
    loads = [(1 << 20) // math.isqrt(rank ** lean) + 1 for rank in range(1, amount + 1)]
    largest = bound if full else min(bound, max(-(-total // amount), total * loads[0] // sum(loads)))
    least = 1 if total - largest >= amount - 1 else 0
    given, surplus = [largest] + [least] * (amount - 1), total - largest - least * (amount - 1)
    while surplus > 0:
        free = [i for i in range(1, amount) if given[i] < largest] or [i for i in range(1, amount) if given[i] < bound]
        whole, left = sum([loads[i] for i in free]), surplus
        for i in free:
            extra = min(bound - given[i], max(1, left * loads[i] // whole), surplus)
            given[i] = given[i] + extra
            surplus = surplus - extra
    return np.array(given)


def gaussian(stream_key, dims, spread, most, pieces=(), kind=jnp.bfloat16):
    entries = spread * jax.random.normal(stream_key, dims, jnp.float32)
    if pieces:
        entries = entries * block_levels(stream_key, dims, pieces, -0.22, 0.18)
    return jnp.clip(entries, -most, most).astype(kind)


def setup_inputs(seed: int = 0) -> dict:
    streams_of = jax.random.split(jax.random.key(seed), 12)
    table_a = gaussian(streams_of[0], (ROWS_A, W_A), 1.0, 6.0, ((0, 64),))
    table_b = gaussian(streams_of[1], (ROWS_B, W_B), 1.0, 6.0, ((0, 64),))
    proj_a = gaussian(streams_of[2], (W_A, E), W_A ** -0.5, 0.75)
    proj_b = gaussian(streams_of[3], (W_B, E), W_B ** -0.5, 1.0)
    owner_a_keys = jax.random.split(jax.random.fold_in(streams_of[4], 1), LOOK_ALL // LOOK)
    owner_a_turns = jax.random.permutation(jax.random.fold_in(streams_of[4], 3), LOOK_ALL // LOOK)
    owner_a = jax.vmap(lambda own, number: assign_block(jax.random.fold_in(streams_of[4], 2), own, number, LOOK, N_SHARD, 1, CAP, 2))(owner_a_keys, owner_a_turns).reshape((LOOK_ALL, 1))
    row_a = place_ends(jax.random.randint(streams_of[5], (LOOK_ALL,), 0, ROWS_DEV), jax.random.fold_in(streams_of[5], 1), 0, ROWS_DEV - 1).astype(jnp.int32)
    bag_a = jax.vmap(lambda own: jnp.searchsorted(jnp.cumsum(uneven_parts(own, BAGS, LOOK, 4, 2)), jnp.arange(LOOK), side="right"))(jax.random.split(streams_of[6], (N_SHARD * N_REP))).reshape((N_SHARD * N_REP, LOOK)).astype(jnp.int32)
    owner_b_keys = jax.random.split(jax.random.fold_in(streams_of[7], 1), LOOK_ALL // LOOK)
    owner_b_turns = jax.random.permutation(jax.random.fold_in(streams_of[7], 3), LOOK_ALL // LOOK)
    owner_b = jax.vmap(lambda own, number: assign_block(jax.random.fold_in(streams_of[7], 2), own, number, LOOK, N_SHARD, 1, CAP, 2))(owner_b_keys, owner_b_turns).reshape((LOOK_ALL, 1))
    row_b = place_ends(jax.random.randint(streams_of[8], (LOOK_ALL,), 0, ROWS_DEV), jax.random.fold_in(streams_of[8], 1), 0, ROWS_DEV - 1).astype(jnp.int32)
    bag_b = jax.vmap(lambda own: jnp.searchsorted(jnp.cumsum(uneven_parts(own, BAGS, LOOK, 4, 2)), jnp.arange(LOOK), side="right"))(jax.random.split(streams_of[9], (N_SHARD * N_REP))).reshape((N_SHARD * N_REP, LOOK)).astype(jnp.int32)
    d_pooled = gaussian(streams_of[10], (BAGS_ALL, E), 1.0, 6.0, ((0, 1024),))
    return {"table_a": table_a, "table_b": table_b, "proj_a": proj_a, "proj_b": proj_b, "owner_a": owner_a, "row_a": row_a, "bag_a": bag_a, "owner_b": owner_b, "row_b": row_b, "bag_b": bag_b, "d_pooled": d_pooled}


def lookup_tier(table, proj, owner, row, bag):
    devices = N_SHARD * N_REP
    device = jnp.arange(LOOK_ALL, dtype=jnp.int32) // LOOK
    global_row = (owner[:, 0] * ROWS_DEV + row).astype(jnp.int32)
    gathered = table[global_row]
    lifted = jnp.dot(gathered, proj, preferred_element_type=jnp.float32).astype(jnp.bfloat16)
    bag_global = (device * BAGS + bag.reshape(-1)).astype(jnp.int32)
    return (gathered, global_row, lifted, bag_global)

def tier_grads(table, proj, gathered, global_row, bag_global, d_pooled):
    lift_grad = d_pooled[bag_global]
    row_grad = jnp.dot(lift_grad, proj.T, preferred_element_type=jnp.float32).astype(jnp.bfloat16)
    grad_table = jax.ops.segment_sum(row_grad.astype(jnp.float32), global_row, table.shape[0])
    grad_proj = jnp.dot(gathered.T, lift_grad, preferred_element_type=jnp.float32)
    grad_proj = grad_proj / jnp.sqrt(jnp.float32(LOOK_ALL))
    return (grad_table, grad_proj)

def reference(table_a, table_b, proj_a, proj_b, owner_a, row_a, bag_a, owner_b, row_b, bag_b, d_pooled):
    total_bags = d_pooled.shape[0]
    gathered_a, global_a, lifted_a, bags_a = lookup_tier(table_a, proj_a, owner_a, row_a, bag_a)
    gathered_b, global_b, lifted_b, bags_b = lookup_tier(table_b, proj_b, owner_b, row_b, bag_b)
    pooled = jax.ops.segment_sum(lifted_a.astype(jnp.float32), bags_a, total_bags)
    pooled = pooled + jax.ops.segment_sum(lifted_b.astype(jnp.float32), bags_b, total_bags)
    pooled = pooled.astype(jnp.bfloat16)
    grad_table_a, grad_proj_a = tier_grads(table_a, proj_a, gathered_a, global_a, bags_a, d_pooled)
    grad_table_b, grad_proj_b = tier_grads(table_b, proj_b, gathered_b, global_b, bags_b, d_pooled)
    return (pooled, grad_table_a, grad_table_b, grad_proj_a, grad_proj_b)
```

```python
import jax
import jax.numpy as jnp
from jax import lax
from jax.sharding import PartitionSpec as P

F32, BF16 = jnp.float32, jnp.bfloat16
BASE = 32


def dot(left, right, dims):
    return lax.dot_general(left, right, (dims, ((), ())), preferred_element_type=F32)


def slot_of(owner, shards, capacity):
    lookups = owner.shape[1]
    named = owner == lax.broadcasted_iota(jnp.int32, (shards, lookups), 0)
    before = lax.broadcasted_iota(jnp.int32, (lookups, lookups), 0) < lax.broadcasted_iota(
        jnp.int32, (lookups, lookups), 1
    )
    earlier = dot(named.astype(BF16), before.astype(BF16), ((1,), (0,)))
    position = jnp.sum(jnp.where(named, earlier, 0.0), axis=0, keepdims=True)
    return owner * capacity + position.astype(jnp.int32)


def onehot_rows(index, count):
    shape = (count, index.shape[1])
    return (index == lax.broadcasted_iota(jnp.int32, shape, 0)).astype(BF16)


def onehot_columns(index, count):
    shape = (index.shape[0], count)
    return (index == lax.broadcasted_iota(jnp.int32, shape, 1)).astype(BF16)


def exchange(x, axis):
    return lax.all_to_all(x, axis, split_axis=0, concat_axis=0, tiled=True)


def spread(x, axis):
    return exchange(jnp.broadcast_to(x[None], (lax.axis_size(axis),) + x.shape), axis)


def body(table_a, table_b, proj_a, proj_b, owner_a, row_a, bag_a, owner_b, row_b, bag_b, d_pooled):
    shards = lax.axis_size("shard")
    replicas = lax.axis_size("rep")
    lookups = row_a.shape[0]
    rows, wide_a = table_a.shape
    wide_b = table_b.shape[1]
    capacity = 3 * lookups // (2 * shards)
    bags, embed = d_pooled.shape
    slots = shards * capacity
    proj = jnp.concatenate([proj_a, proj_b], axis=0)
    row_grad = dot(proj, d_pooled, ((1,), (1,))).astype(BF16)
    held_a = onehot_rows(slot_of(owner_a.reshape(1, lookups), shards, capacity), slots)
    held_b = onehot_rows(slot_of(owner_b.reshape(1, lookups), shards, capacity), slots)
    bag_a, bag_b = onehot_rows(bag_a, bags), onehot_rows(bag_b, bags)
    row_a, row_b = row_a.reshape(1, lookups), row_b.reshape(1, lookups)
    none = lambda count: jnp.zeros((count, lookups), BF16)
    sent_a = jnp.concatenate(
        [
            dot(row_grad[:wide_a], bag_a, ((1,), (0,))).astype(BF16),
            none(wide_b),
            (row_a // BASE).astype(BF16),
            (row_a % BASE).astype(BF16),
            none(128 - wide_a - wide_b - 2),
        ]
    )
    sent_b = jnp.concatenate(
        [
            none(wide_a),
            dot(row_grad[wide_a:], bag_b, ((1,), (0,))).astype(BF16),
            none(2),
            (row_b // BASE).astype(BF16),
            (row_b % BASE).astype(BF16),
            none(128 - wide_a - wide_b - 4),
        ]
    )
    sent = dot(held_a, sent_a, ((1,), (1,))) + dot(held_b, sent_b, ((1,), (1,)))
    came = exchange(sent.astype(BF16).reshape(shards, capacity, 128), "shard").reshape(slots, 128)
    wanted = came[:, wide_a + wide_b : wide_a + wide_b + 4].astype(jnp.int32)
    row_hot_a = onehot_columns(wanted[:, 0:1] * BASE + wanted[:, 1:2], rows)
    row_hot_b = onehot_columns(wanted[:, 2:3] * BASE + wanted[:, 3:4], rows)
    gathered = jnp.concatenate(
        [
            dot(row_hot_a, table_a, ((1,), (0,))).astype(BF16),
            dot(row_hot_b, table_b, ((1,), (0,))).astype(BF16),
            jnp.zeros((slots, 128 - wide_a - wide_b), BF16),
        ],
        axis=1,
    )
    back = exchange(gathered.reshape(shards, capacity, 128), "shard").reshape(slots, 128)
    grads = jnp.concatenate(
        [
            dot(came[:, :wide_a], row_hot_a, ((0,), (0,))),
            dot(came[:, wide_a : wide_a + wide_b], row_hot_b, ((0,), (0,))),
        ]
    ).astype(BF16)
    wide = wide_a + wide_b
    pieces = grads.reshape(wide, replicas, rows // replicas).transpose(1, 0, 2)
    share = jnp.sum(exchange(pieces, "rep").astype(F32), axis=0).astype(BF16)
    grads = spread(share, "rep").transpose(1, 0, 2).reshape(wide, rows).astype(F32)
    looked_a = dot(back[:, :wide_a], held_a, ((0,), (0,))).astype(BF16)
    looked_b = dot(back[:, wide_a:wide], held_b, ((0,), (0,))).astype(BF16)
    summed = jnp.concatenate([dot(looked_a, bag_a, ((1,), (1,))), dot(looked_b, bag_b, ((1,), (1,)))])
    high = summed.astype(BF16)
    low = (summed - high.astype(F32)).astype(BF16)
    pooled = dot(high, proj, ((0,), (0,))) + dot(low, proj, ((0,), (0,)))
    partial = dot(high, d_pooled, ((1,), (0,))) + dot(low, d_pooled, ((1,), (0,)))
    part = jnp.sum(exchange(partial.reshape(shards, -1), "shard"), axis=0)
    part = jnp.sum(spread(part, "rep"), axis=0)
    part = part / jnp.sqrt(F32(lookups * shards * replicas))
    grad_proj = spread(part, "shard").reshape(wide, embed)
    return (
        pooled.astype(BF16),
        grads[:wide_a].T,
        grads[wide_a:].T,
        grad_proj[:wide_a],
        grad_proj[wide_a:],
    )


def solution(mesh):
    split = ("shard", "rep")
    tier = (P(split, None), P(split), P(split, None))
    in_specs = (P("shard", None), P("shard", None), P(), P(), *tier, *tier, P(split, None))
    out_specs = (P(split, None), P("shard", None), P("shard", None), P(), P())
    return jax.shard_map(body, mesh=mesh, in_specs=in_specs, out_specs=out_specs, check_vma=False)
```

```python
import functools

import jax
import jax.numpy as jnp
from jax import lax
from jax.experimental import pallas as pl
from jax.experimental.pallas import tpu as pltpu
from jax.sharding import PartitionSpec as P

F32, BF16, I32 = jnp.float32, jnp.bfloat16, jnp.int32
LANES = 128
SLOT_ROWS = 32
GROUPS = 8
DIGIT = 5


def dot(left, right, dims=((1,), (0,))):
    return lax.dot_general(left, right, (dims, ((), ())), preferred_element_type=F32)


def iota(shape, dim):
    return lax.broadcasted_iota(I32, shape, dim)


def onehot(hit):
    return jnp.where(hit, 1.0, 0.0).astype(BF16)


def wait_bytes(ref, sem):
    pltpu.make_async_copy(ref, ref, sem).wait()


def digits(row, first, shape):
    at = iota(shape, 0)
    high, low = lax.shift_right_logical(row, DIGIT), jnp.bitwise_and(row, (1 << DIGIT) - 1)
    return jnp.where(at == first, high, jnp.where(at == first + 1, low, 0))


def column(block, lane):
    at = iota((1, LANES), 1)
    weight = jnp.where(at == lane, float(1 << DIGIT), jnp.where(at == lane + 1, 1.0, 0.0))
    return jnp.sum(block * weight, axis=1, keepdims=True).astype(I32)


def order(step, start):
    odd = step % 2
    return (start + 4 + (1 - odd) * (step // 2) - odd * ((step + 1) // 2) + GROUPS) % GROUPS


def kernel(
    shards,
    replicas,
    tab_a, tab_b, proj_a, proj_b, owner_a, row_a, bag_a, owner_b, row_b, bag_b, d_pooled,
    pooled_out, grads_out, proj_out,
    tabs, proj, slot, give, sent, came, found, back, bags_a, bags_b, grads, looked,
    piece, piece_in, share, share_in, part, part_in, tile, tile_in, done, done_in,
    local_sem, send_sems, came_sems, back_sems, recv_sems,
):
    me, rep = lax.axis_index("shard"), lax.axis_index("rep")
    lookups, rows, bags = owner_a.shape[1], tab_a.shape[1], d_pooled.shape[0]
    wide_a, wide_b = tab_a.shape[0], tab_b.shape[0]
    wide = wide_a + wide_b
    per_group = shards // GROUPS
    slots = per_group * SLOT_ROWS
    my_group = me // per_group
    holders, per = part.shape[0], part.shape[1] // 8
    stride = shards // holders

    barrier = pltpu.get_barrier_semaphore()

    def greet_shard(step, carry):
        pl.semaphore_signal(barrier, inc=1, device_id=((me + step) % shards, rep), device_id_type=pl.DeviceIdType.MESH)
        return carry

    def greet_rep(step, carry):
        pl.semaphore_signal(barrier, inc=1, device_id=(me, (rep + step) % replicas), device_id_type=pl.DeviceIdType.MESH)
        return carry

    lax.fori_loop(1, shards, greet_shard, 0)
    lax.fori_loop(1, replicas, greet_rep, 0)

    proj[0:wide_a, :] = proj_a[...]
    proj[wide_a:wide, :] = proj_b[...]
    proj[wide:, :] = jnp.zeros((LANES - wide, proj.shape[1]), BF16)
    tabs[...] = jnp.zeros_like(tabs)
    tabs[0, 0:wide_a, :] = tab_a[...]
    tabs[1, wide_a:wide, :] = tab_b[...]
    give[...] = jnp.zeros_like(give)

    row_grad = dot(proj[...], d_pooled[...], ((1,), (1,))).astype(BF16)
    chunk = min(256, lookups)
    before = onehot(iota((chunk, chunk), 0) < iota((chunk, chunk), 1))
    carried = jnp.zeros((2 * shards, 1), F32)
    for first in range(0, lookups, chunk):
        cut = slice(first, first + chunk)
        named_a = owner_a[:, cut] == iota((shards, chunk), 0)
        named_b = owner_b[:, cut] == iota((shards, chunk), 0)
        named = jnp.concatenate([jnp.where(named_a, 1.0, 0.0), jnp.where(named_b, 1.0, 0.0)])
        earlier = dot(named.astype(BF16), before) + carried
        carried = carried + jnp.sum(named, axis=1, keepdims=True)
        earlier = earlier * named
        place_a = jnp.sum(earlier[:shards], axis=0, keepdims=True).astype(I32)
        place_b = jnp.sum(earlier[shards:], axis=0, keepdims=True).astype(I32)
        slot[0:1, cut] = owner_a[:, cut] * SLOT_ROWS + place_a
        slot[1:2, cut] = owner_b[:, cut] * SLOT_ROWS + place_b
        in_bag = onehot(bag_a[:, cut] == iota((bags, chunk), 0))
        give[0, 0:wide_a, cut] = dot(row_grad[0:wide_a], in_bag).astype(BF16)
        in_bag = onehot(bag_b[:, cut] == iota((bags, chunk), 0))
        give[1, wide_a:wide, cut] = dot(row_grad[wide_a:wide], in_bag).astype(BF16)
        tail = (LANES - wide, chunk)
        give[0, wide:, cut] = (digits(row_a[:, cut], 0, tail) + digits(bag_a[:, cut] + 1, 2, tail)).astype(F32).astype(BF16)
        give[1, wide:, cut] = (digits(row_b[:, cut], 4, tail) + digits(bag_b[:, cut] + 1, 6, tail)).astype(F32).astype(BF16)

    pl.semaphore_wait(barrier, shards + replicas - 2)

    def to_shard(block, there, target, send_sem, recv_sem):
        pltpu.make_async_remote_copy(
            src_ref=block,
            dst_ref=there,
            send_sem=send_sem,
            recv_sem=recv_sem,
            device_id=(target, rep),
            device_id_type=pl.DeviceIdType.MESH,
        ).start()

    def to_rep(block, there, target, send_sem, recv_sem):
        pltpu.make_async_remote_copy(
            src_ref=block,
            dst_ref=there,
            send_sem=send_sem,
            recv_sem=recv_sem,
            device_id=(me, target),
            device_id_type=pl.DeviceIdType.MESH,
        ).start()

    def send_group(group, source, landing, send_sem, recv_sem):
        def one(i, carry):
            target = group * per_group + i

            @pl.when(target != me)
            def _():
                to_shard(source.at[target], landing.at[me], target, send_sem, recv_sem)

            @pl.when(target == me)
            def _():
                pltpu.make_async_copy(source.at[target], landing.at[me], recv_sem).start()

            return carry

        lax.fori_loop(0, per_group, one, 0)

    def ask(step, carry):
        group = order(step, my_group)
        at = iota((slots, lookups), 0) + group * slots
        block = dot(onehot(slot[0:1, :] == at), give[0], ((1,), (1,)))
        block += dot(onehot(slot[1:2, :] == at), give[1], ((1,), (1,)))
        sent[pl.ds(group * per_group, per_group)] = block.reshape(per_group, SLOT_ROWS, LANES).astype(BF16)
        send_group(group, sent, came, send_sems.at[0], came_sems.at[my_group])
        return carry

    lax.fori_loop(0, GROUPS, ask, 0)

    grads[...] = jnp.zeros_like(grads)
    looked[...] = jnp.zeros_like(looked)

    def mark(group, carry):
        block = sent[pl.ds(group * per_group, per_group)].reshape(slots, LANES).astype(F32)
        at = iota((slots, bags), 1) + 1
        bags_a[pl.ds(group * slots, slots), :] = onehot(column(block, wide + 2) == at)
        bags_b[pl.ds(group * slots, slots), :] = onehot(column(block, wide + 6) == at)
        return carry

    lax.fori_loop(0, GROUPS, mark, 0)

    def answer(step, carry):
        group = order(step, my_group)
        mine = pl.ds(group * per_group, per_group)
        wait_bytes(came.at[mine], came_sems.at[group])
        block = came[mine].reshape(slots, LANES).astype(F32)
        at = iota((slots, rows), 1)
        hot_a = onehot(column(block, wide) == at)
        hot_b = onehot(column(block, wide + 4) == at)
        gathered = dot(hot_a, tabs[0], ((1,), (1,))) + dot(hot_b, tabs[1], ((1,), (1,)))
        found[mine] = gathered.reshape(per_group, SLOT_ROWS, LANES).astype(BF16)
        send_group(group, found, back, send_sems.at[1], back_sems.at[my_group])
        turned = block.T.astype(BF16)
        grads[0:wide_a, :] += dot(turned[0:wide_a], hot_a)
        grads[wide_a:wide, :] += dot(turned[wide_a:wide], hot_b)
        return carry

    lax.fori_loop(0, GROUPS, answer, 0)

    tall, broad = piece.shape[1], piece.shape[2]
    across = rows // broad
    for k in range(replicas):
        high, left = (k // across) * tall, (k % across) * broad
        piece[k] = grads[high : high + tall, left : left + broad].astype(BF16)
    piece_in[rep] = piece[rep]

    def scatter(step, carry):
        target = (rep + step) % replicas
        to_rep(piece.at[target], piece_in.at[rep], target, send_sems.at[2], recv_sems.at[0])
        return carry

    lax.fori_loop(1, replicas, scatter, 0)

    def pool(step, carry):
        group = order(step, my_group)
        mine = pl.ds(group * per_group, per_group)
        wait_bytes(back.at[mine], back_sems.at[group])
        turned = back[mine].reshape(slots, LANES).astype(F32).T.astype(BF16)
        here = pl.ds(group * slots, slots)
        looked[0:wide_a, :] += dot(turned[0:wide_a], bags_a[here, :])
        looked[wide_a:wide, :] += dot(turned[wide_a:wide], bags_b[here, :])
        return carry

    lax.fori_loop(0, GROUPS, pool, 0)

    high = looked[...].astype(BF16)
    low = (looked[...] - high.astype(F32)).astype(BF16)
    partial = dot(high, d_pooled[...]) + dot(low, d_pooled[...])
    embed = partial.shape[1]
    halves = embed // LANES
    for k in range(holders * per):
        top, left = (k // halves) * 8, (k % halves) * LANES
        part[k // per, (k % per) * 8 : (k % per) * 8 + 8, :] = partial[top : top + 8, left : left + LANES]
    index = me // stride
    holding = jnp.logical_and(me == index * stride, index < holders)

    def hand(step, carry):
        target = (index + step) % holders

        @pl.when(target * stride != me)
        def _():
            to_shard(part.at[target], part_in.at[me], target * stride, send_sems.at[4], recv_sems.at[2])

        return carry

    lax.fori_loop(0, holders, hand, 0)

    wait_bytes(piece_in.at[pl.ds(0, replicas - 1)], recv_sems.at[0])
    share[...] = jnp.sum(piece_in[...].astype(F32), axis=0).astype(BF16)
    share_in[rep] = share[...]

    def give_share(step, carry):
        to_rep(share, share_in.at[rep], (rep + step) % replicas, send_sems.at[3], recv_sems.at[1])
        return carry

    lax.fori_loop(1, replicas, give_share, 0)

    @pl.when(holding)
    def _():
        part_in[me] = part[index]
        wait_bytes(part_in.at[pl.ds(0, shards - 1)], recv_sems.at[2])
        tile[...] = jnp.sum(part_in[...], axis=0)
        tile_in[rep] = tile[...]

        def swap(step, carry):
            to_rep(tile, tile_in.at[rep], (rep + step) % replicas, send_sems.at[5], recv_sems.at[3])
            return carry

        lax.fori_loop(1, replicas, swap, 0)

    turned = looked[...].T
    high = turned.astype(BF16)
    low = (turned - high.astype(F32)).astype(BF16)
    pooled_out[...] = (dot(high, proj[...]) + dot(low, proj[...])).astype(BF16)

    @pl.when(holding)
    def _():
        wait_bytes(tile_in.at[pl.ds(0, replicas - 1)], recv_sems.at[3])
        scale = 1.0 / (float(lookups * shards * replicas) ** 0.5)
        done[...] = jnp.sum(tile_in[...], axis=0) * scale
        done_in[index] = done[...]

        def tell(step, carry):
            to_shard(done, done_in.at[index], (me + step) % shards, send_sems.at[6], recv_sems.at[4])
            return carry

        lax.fori_loop(1, shards, tell, 0)

    wait_bytes(share_in.at[pl.ds(0, replicas - 1)], recv_sems.at[1])
    for k in range(replicas):
        top, left = (k // across) * tall, (k % across) * broad
        grads_out[top : top + tall, left : left + broad] = share_in[k]

    @pl.when(holding)
    def _():
        wait_bytes(done_in.at[pl.ds(0, holders - 1)], recv_sems.at[4])

    @pl.when(jnp.logical_not(holding))
    def _():
        wait_bytes(done_in, recv_sems.at[4])

    for k in range(holders * per):
        top, left = (k // halves) * 8, (k % halves) * LANES
        proj_out[top : top + 8, left : left + LANES] = done_in[k // per, (k % per) * 8 : (k % per) * 8 + 8, :]

    wait_bytes(sent.at[pl.ds(0, shards - 1)], send_sems.at[0])
    wait_bytes(found.at[pl.ds(0, shards - 1)], send_sems.at[1])
    wait_bytes(piece.at[pl.ds(0, replicas - 1)], send_sems.at[2])
    wait_bytes(share_in.at[pl.ds(0, replicas - 1)], send_sems.at[3])

    @pl.when(holding)
    def _():
        wait_bytes(part.at[pl.ds(0, holders - 1)], send_sems.at[4])
        wait_bytes(tile_in.at[pl.ds(0, replicas - 1)], send_sems.at[5])
        wait_bytes(part_in.at[pl.ds(0, shards - 1)], send_sems.at[6])

    @pl.when(jnp.logical_not(holding))
    def _():
        wait_bytes(part, send_sems.at[4])


def body(table_a, table_b, proj_a, proj_b, owner_a, row_a, bag_a, owner_b, row_b, bag_b, d_pooled):
    shards, replicas = lax.axis_size("shard"), lax.axis_size("rep")
    lookups = row_a.shape[0]
    rows, wide_a = table_a.shape
    wide = wide_a + table_b.shape[1]
    bags, embed = d_pooled.shape
    tiles = wide * embed // (8 * LANES)
    holders = min(tiles, shards)
    per = tiles // holders
    tall, broad = wide // 2, 2 * rows // replicas
    block = pltpu.VMEM((shards, SLOT_ROWS, LANES), BF16)
    line = (1, lookups)
    pooled, grads, grad_proj = pl.pallas_call(
        functools.partial(kernel, shards, replicas),
        out_shape=(
            jax.ShapeDtypeStruct((bags, embed), BF16),
            jax.ShapeDtypeStruct((wide, rows), BF16),
            jax.ShapeDtypeStruct((wide, embed), F32),
        ),
        in_specs=[pl.BlockSpec(memory_space=pltpu.VMEM)] * 11,
        out_specs=(pl.BlockSpec(memory_space=pltpu.VMEM),) * 3,
        scratch_shapes=[
            pltpu.VMEM((2, LANES, rows), BF16),
            pltpu.VMEM((LANES, embed), BF16),
            pltpu.VMEM((8, lookups), I32),
            pltpu.VMEM((2, LANES, lookups), BF16),
            block,
            block,
            block,
            block,
            pltpu.VMEM((shards * SLOT_ROWS, bags), BF16),
            pltpu.VMEM((shards * SLOT_ROWS, bags), BF16),
            pltpu.VMEM((wide, rows), F32),
            pltpu.VMEM((LANES, bags), F32),
            pltpu.VMEM((replicas, tall, broad), BF16),
            pltpu.VMEM((replicas, tall, broad), BF16),
            pltpu.VMEM((tall, broad), BF16),
            pltpu.VMEM((replicas, tall, broad), BF16),
            pltpu.VMEM((holders, 8 * per, LANES), F32),
            pltpu.VMEM((shards, 8 * per, LANES), F32),
            pltpu.VMEM((8 * per, LANES), F32),
            pltpu.VMEM((replicas, 8 * per, LANES), F32),
            pltpu.VMEM((8 * per, LANES), F32),
            pltpu.VMEM((holders, 8 * per, LANES), F32),
            pltpu.SemaphoreType.DMA((1,)),
            pltpu.SemaphoreType.DMA((7,)),
            pltpu.SemaphoreType.DMA((GROUPS,)),
            pltpu.SemaphoreType.DMA((GROUPS,)),
            pltpu.SemaphoreType.DMA((5,)),
        ],
        compiler_params=pltpu.CompilerParams(
            collective_id=0, has_side_effects=True, vmem_limit_bytes=48 * 1024 * 1024
        ),
    )(
        table_a.T,
        table_b.T,
        proj_a,
        proj_b,
        owner_a.reshape(line),
        row_a.reshape(line),
        bag_a,
        owner_b.reshape(line),
        row_b.reshape(line),
        bag_b,
        d_pooled,
    )
    grads = grads.astype(F32).T
    return (pooled, grads[:, :wide_a], grads[:, wide_a:], grad_proj[:wide_a], grad_proj[wide_a:])


def solution(mesh):
    split = ("shard", "rep")
    tier = (P(split, None), P(split), P(split, None))
    in_specs = (P("shard", None), P("shard", None), P(), P(), *tier, *tier, P(split, None))
    out_specs = (P(split, None), P("shard", None), P("shard", None), P(), P())
    return jax.shard_map(body, mesh=mesh, in_specs=in_specs, out_specs=out_specs, check_vma=False)
```

```python
import functools

import jax
import jax.numpy as jnp
from jax import lax
from jax.experimental import pallas as pl
from jax.experimental.pallas import tpu as pltpu
from jax.sharding import PartitionSpec as P

F32, BF16, I32 = jnp.float32, jnp.bfloat16, jnp.int32
LANES = 128
SLOT_ROWS = 24
GROUPS = 8
DIGIT = 5
VMEM = 64 * 1024 * 1024


def dot(left, right, dims=((1,), (0,))):
    return lax.dot_general(left, right, (dims, ((), ())), preferred_element_type=F32)


def iota(shape, dim):
    return lax.broadcasted_iota(I32, shape, dim)


def onehot(hit):
    return jnp.where(hit, 1.0, 0.0).astype(BF16)


def wait_bytes(ref, sem):
    pltpu.make_async_copy(ref, ref, sem).wait()


def digits(row, first, shape):
    at = iota(shape, 0)
    high, low = lax.shift_right_logical(row, DIGIT), jnp.bitwise_and(row, (1 << DIGIT) - 1)
    return jnp.where(at == first, high, jnp.where(at == first + 1, low, 0))


def column(block, lane):
    at = iota((1, LANES), 1)
    weight = jnp.where(at == lane, float(1 << DIGIT), jnp.where(at == lane + 1, 1.0, 0.0))
    return jnp.sum(block * weight, axis=1, keepdims=True).astype(I32)


def order(step, start):
    odd = step % 2
    return (start + 4 + (1 - odd) * (step // 2) - odd * ((step + 1) // 2) + GROUPS) % GROUPS


def kernel(
    shards,
    replicas,
    tab_a, tab_b, proj_a, proj_b, owner_a_in, row_a_in, bag_a_in, owner_b_in, row_b_in, bag_b_in, d_pooled_in,
    pooled_out, grads_out, proj_out,
    owner_a, row_a, bag_a, owner_b, row_b, bag_b, d_pooled,
    tabs, proj, slot, give, sent, came, found, back, bags_a, bags_b, grads, looked,
    piece, piece_in, share, share_in, part, part_in, tile, tile_in, done, done_in,
    in_sems, send_sems, came_sems, back_sems, recv_sems,
):
    me, rep = lax.axis_index("shard"), lax.axis_index("rep")
    lookups, rows, bags = owner_a.shape[1], tab_a.shape[1], d_pooled.shape[0]
    wide_a, wide_b = tab_a.shape[0], tab_b.shape[0]
    wide = wide_a + wide_b
    per_group = shards // GROUPS
    slots = per_group * SLOT_ROWS
    my_group = me // per_group
    holders, per = part.shape[0], part.shape[1] // 8
    stride = shards // holders

    loads = [
        pltpu.make_async_copy(source, target, in_sems.at[k])
        for k, (source, target) in enumerate(
            (
                (owner_a_in, owner_a),
                (owner_b_in, owner_b),
                (bag_a_in, bag_a),
                (bag_b_in, bag_b),
                (row_a_in, row_a),
                (row_b_in, row_b),
                (proj_a, proj.at[0:wide_a]),
                (proj_b, proj.at[wide_a:wide]),
                (d_pooled_in, d_pooled),
                (tab_a, tabs.at[0, 0:wide_a]),
                (tab_b, tabs.at[1, wide_a:wide]),
            )
        )
    ]
    for load in loads:
        load.start()
    barrier = pltpu.get_barrier_semaphore()

    def greet_shard(step, carry):
        pl.semaphore_signal(barrier, inc=1, device_id=((me + step) % shards, rep), device_id_type=pl.DeviceIdType.MESH)
        return carry

    def greet_rep(step, carry):
        pl.semaphore_signal(barrier, inc=1, device_id=(me, (rep + step) % replicas), device_id_type=pl.DeviceIdType.MESH)
        return carry

    lax.fori_loop(1, shards, greet_shard, 0)
    lax.fori_loop(1, replicas, greet_rep, 0)

    proj[wide:, :] = jnp.zeros((LANES - wide, proj.shape[1]), BF16)
    tabs[0, wide_a:, :] = jnp.zeros((LANES - wide_a, rows), BF16)
    tabs[1, 0:wide_a, :] = jnp.zeros((wide_a, rows), BF16)
    tabs[1, wide:, :] = jnp.zeros((LANES - wide, rows), BF16)
    give[0, wide_a:wide, :] = jnp.zeros((wide - wide_a, lookups), BF16)
    give[1, 0:wide_a, :] = jnp.zeros((wide_a, lookups), BF16)
    for load in loads[:9]:
        load.wait()

    row_grad = dot(proj[...], d_pooled[...], ((1,), (1,))).astype(BF16)
    chunk = min(256, lookups)
    before = onehot(iota((chunk, chunk), 0) < iota((chunk, chunk), 1))
    carried = jnp.zeros((2 * shards, 1), F32)
    for first in range(0, lookups, chunk):
        cut = slice(first, first + chunk)
        named_a = owner_a[:, cut] == iota((shards, chunk), 0)
        named_b = owner_b[:, cut] == iota((shards, chunk), 0)
        named = jnp.concatenate([jnp.where(named_a, 1.0, 0.0), jnp.where(named_b, 1.0, 0.0)])
        earlier = dot(named.astype(BF16), before) + carried
        carried = carried + jnp.sum(named, axis=1, keepdims=True)
        earlier = earlier * named
        place_a = jnp.sum(earlier[:shards], axis=0, keepdims=True).astype(I32)
        place_b = jnp.sum(earlier[shards:], axis=0, keepdims=True).astype(I32)
        slot[0:1, cut] = owner_a[:, cut] * SLOT_ROWS + place_a
        slot[1:2, cut] = owner_b[:, cut] * SLOT_ROWS + place_b
        in_bag = onehot(bag_a[:, cut] == iota((bags, chunk), 0))
        give[0, 0:wide_a, cut] = dot(row_grad[0:wide_a], in_bag).astype(BF16)
        in_bag = onehot(bag_b[:, cut] == iota((bags, chunk), 0))
        give[1, wide_a:wide, cut] = dot(row_grad[wide_a:wide], in_bag).astype(BF16)
        tail = (LANES - wide, chunk)
        give[0, wide:, cut] = (digits(row_a[:, cut], 0, tail) + digits(bag_a[:, cut] + 1, 2, tail)).astype(F32).astype(BF16)
        give[1, wide:, cut] = (digits(row_b[:, cut], 4, tail) + digits(bag_b[:, cut] + 1, 6, tail)).astype(F32).astype(BF16)

    pl.semaphore_wait(barrier, shards + replicas - 2)

    def to_shard(block, there, target, send_sem, recv_sem):
        pltpu.make_async_remote_copy(
            src_ref=block,
            dst_ref=there,
            send_sem=send_sem,
            recv_sem=recv_sem,
            device_id=(target, rep),
            device_id_type=pl.DeviceIdType.MESH,
        ).start()

    def to_rep(block, there, target, send_sem, recv_sem):
        pltpu.make_async_remote_copy(
            src_ref=block,
            dst_ref=there,
            send_sem=send_sem,
            recv_sem=recv_sem,
            device_id=(me, target),
            device_id_type=pl.DeviceIdType.MESH,
        ).start()

    def send_group(group, source, landing, send_sem, recv_sem):
        def one(i, carry):
            target = group * per_group + i

            @pl.when(target != me)
            def _():
                to_shard(source.at[target], landing.at[me], target, send_sem, recv_sem)

            @pl.when(target == me)
            def _():
                pltpu.make_async_copy(source.at[target], landing.at[me], recv_sem).start()

            return carry

        lax.fori_loop(0, per_group, one, 0)

    def ask(step, carry):
        group = order(step, my_group)
        at = iota((slots, lookups), 0) + group * slots
        block = dot(onehot(slot[0:1, :] == at), give[0], ((1,), (1,)))
        block += dot(onehot(slot[1:2, :] == at), give[1], ((1,), (1,)))
        sent[pl.ds(group * per_group, per_group)] = block.reshape(per_group, SLOT_ROWS, LANES).astype(BF16)
        send_group(group, sent, came, send_sems.at[0], came_sems.at[my_group])
        return carry

    lax.fori_loop(0, GROUPS, ask, 0)

    grads[...] = jnp.zeros_like(grads)
    looked[...] = jnp.zeros_like(looked)

    for load in loads[9:]:
        load.wait()

    def answer(step, carry):
        group = order(step, my_group)
        mine = pl.ds(group * per_group, per_group)
        wait_bytes(came.at[mine], came_sems.at[group])
        block = came[mine].astype(F32).reshape(slots, LANES)
        at = iota((slots, rows), 1)
        hot_a = onehot(column(block, wide) == at)
        hot_b = onehot(column(block, wide + 4) == at)
        gathered = dot(hot_a, tabs[0], ((1,), (1,))) + dot(hot_b, tabs[1], ((1,), (1,)))
        found[mine] = gathered.reshape(per_group, SLOT_ROWS, LANES).astype(BF16)
        send_group(group, found, back, send_sems.at[1], back_sems.at[my_group])
        turned = block.T.astype(BF16)
        grads[0:wide_a, :] += dot(turned[0:wide_a], hot_a)
        grads[wide_a:wide, :] += dot(turned[wide_a:wide], hot_b)
        return carry

    lax.fori_loop(0, GROUPS, answer, 0)

    tall, broad = piece.shape[1], piece.shape[2]
    across = rows // broad
    for k in range(replicas):
        high, left = (k // across) * tall, (k % across) * broad
        piece[k] = grads[high : high + tall, left : left + broad].astype(BF16)
    piece_in[rep] = piece[rep]

    def scatter(step, carry):
        target = (rep + step) % replicas
        to_rep(piece.at[target], piece_in.at[rep], target, send_sems.at[2], recv_sems.at[0])
        return carry

    lax.fori_loop(1, replicas, scatter, 0)

    def mark(group, carry):
        block = sent[pl.ds(group * per_group, per_group)].astype(F32).reshape(slots, LANES)
        at = iota((slots, bags), 1) + 1
        bags_a[pl.ds(group * slots, slots), :] = onehot(column(block, wide + 2) == at)
        bags_b[pl.ds(group * slots, slots), :] = onehot(column(block, wide + 6) == at)
        return carry

    lax.fori_loop(0, GROUPS, mark, 0)

    def pool(step, carry):
        group = order(step, my_group)
        mine = pl.ds(group * per_group, per_group)
        wait_bytes(back.at[mine], back_sems.at[group])
        turned = back[mine].astype(F32).reshape(slots, LANES).T.astype(BF16)
        here = pl.ds(group * slots, slots)
        looked[0:wide_a, :] += dot(turned[0:wide_a], bags_a[here, :])
        looked[wide_a:wide, :] += dot(turned[wide_a:wide], bags_b[here, :])
        return carry

    lax.fori_loop(0, GROUPS, pool, 0)

    high = looked[...].astype(BF16)
    low = (looked[...] - high.astype(F32)).astype(BF16)
    partial = dot(high, d_pooled[...]) + dot(low, d_pooled[...])
    embed = partial.shape[1]
    halves = embed // LANES
    for k in range(holders * per):
        top, left = (k // halves) * 8, (k % halves) * LANES
        part[k // per, (k % per) * 8 : (k % per) * 8 + 8, :] = partial[top : top + 8, left : left + LANES]
    index = me // stride
    holding = jnp.logical_and(me == index * stride, index < holders)

    def hand(step, carry):
        target = (index + step) % holders

        @pl.when(target * stride != me)
        def _():
            to_shard(part.at[target], part_in.at[me], target * stride, send_sems.at[4], recv_sems.at[2])

        return carry

    lax.fori_loop(0, holders, hand, 0)

    @pl.when(holding)
    def _():
        part_in[me] = part[index]
        wait_bytes(part_in.at[pl.ds(0, shards - 1)], recv_sems.at[2])
        tile[...] = jnp.sum(part_in[...], axis=0)
        tile_in[rep] = tile[...]

        def swap(step, carry):
            to_rep(tile, tile_in.at[rep], (rep + step) % replicas, send_sems.at[5], recv_sems.at[3])
            return carry

        lax.fori_loop(1, replicas, swap, 0)

    wait_bytes(piece_in.at[pl.ds(0, replicas - 1)], recv_sems.at[0])
    share[...] = jnp.sum(piece_in[...].astype(F32), axis=0).astype(BF16)
    share_in[rep] = share[...]

    def give_share(step, carry):
        to_rep(share, share_in.at[rep], (rep + step) % replicas, send_sems.at[3], recv_sems.at[1])
        return carry

    lax.fori_loop(1, replicas, give_share, 0)

    @pl.when(holding)
    def _():
        wait_bytes(tile_in.at[pl.ds(0, replicas - 1)], recv_sems.at[3])
        scale = 1.0 / (float(lookups * shards * replicas) ** 0.5)
        done[...] = jnp.sum(tile_in[...], axis=0) * scale
        done_in[index] = done[...]

        def tell(step, carry):
            to_shard(done, done_in.at[index], (me + step) % shards, send_sems.at[6], recv_sems.at[4])
            return carry

        lax.fori_loop(1, shards, tell, 0)

    turned = looked[...].T
    high = turned.astype(BF16)
    low = (turned - high.astype(F32)).astype(BF16)
    pooled_out[...] = (dot(high, proj[...]) + dot(low, proj[...])).astype(BF16)

    wait_bytes(share_in.at[pl.ds(0, replicas - 1)], recv_sems.at[1])
    for k in range(replicas):
        top, left = (k // across) * tall, (k % across) * broad
        grads_out[top : top + tall, left : left + broad] = share_in[k]

    @pl.when(holding)
    def _():
        wait_bytes(done_in.at[pl.ds(0, holders - 1)], recv_sems.at[4])

    @pl.when(jnp.logical_not(holding))
    def _():
        wait_bytes(done_in, recv_sems.at[4])

    for k in range(holders * per):
        top, left = (k // halves) * 8, (k % halves) * LANES
        proj_out[top : top + 8, left : left + LANES] = done_in[k // per, (k % per) * 8 : (k % per) * 8 + 8, :]

    wait_bytes(sent.at[pl.ds(0, shards - 1)], send_sems.at[0])
    wait_bytes(found.at[pl.ds(0, shards - 1)], send_sems.at[1])
    wait_bytes(piece.at[pl.ds(0, replicas - 1)], send_sems.at[2])
    wait_bytes(share_in.at[pl.ds(0, replicas - 1)], send_sems.at[3])

    @pl.when(holding)
    def _():
        wait_bytes(part.at[pl.ds(0, holders - 1)], send_sems.at[4])
        wait_bytes(tile_in.at[pl.ds(0, replicas - 1)], send_sems.at[5])
        wait_bytes(part_in.at[pl.ds(0, shards - 1)], send_sems.at[6])

    @pl.when(jnp.logical_not(holding))
    def _():
        wait_bytes(part, send_sems.at[4])


def finish(pooled, grads, grad_proj, pooled_out, grad_a, grad_b, proj_a, proj_b):
    wide_a = grad_a.shape[0]
    pooled_out[...] = pooled[...]
    grad_a[...] = grads[0:wide_a, :].astype(F32)
    grad_b[...] = grads[wide_a:, :].astype(F32)
    proj_a[...] = grad_proj[0:wide_a, :]
    proj_b[...] = grad_proj[wide_a:, :]


def body(table_a, table_b, proj_a, proj_b, owner_a, row_a, bag_a, owner_b, row_b, bag_b, d_pooled):
    shards, replicas = lax.axis_size("shard"), lax.axis_size("rep")
    lookups = row_a.shape[0]
    rows, wide_a = table_a.shape
    wide = wide_a + table_b.shape[1]
    bags, embed = d_pooled.shape
    tiles = wide * embed // (8 * LANES)
    holders = min(tiles, shards)
    per = tiles // holders
    tall, broad = wide // 2, 2 * rows // replicas
    block = pltpu.VMEM((shards, SLOT_ROWS, LANES), BF16)
    line = (1, lookups)
    pooled, grads, grad_proj = pl.pallas_call(
        functools.partial(kernel, shards, replicas),
        out_shape=(
            jax.ShapeDtypeStruct((bags, embed), BF16),
            jax.ShapeDtypeStruct((wide, rows), BF16),
            jax.ShapeDtypeStruct((wide, embed), F32),
        ),
        in_specs=[pl.BlockSpec(memory_space=pltpu.HBM)] * 11,
        out_specs=(pl.BlockSpec(memory_space=pltpu.VMEM),) * 3,
        scratch_shapes=[
            pltpu.VMEM(line, I32),
            pltpu.VMEM(line, I32),
            pltpu.VMEM(line, I32),
            pltpu.VMEM(line, I32),
            pltpu.VMEM(line, I32),
            pltpu.VMEM(line, I32),
            pltpu.VMEM((bags, embed), BF16),
            pltpu.VMEM((2, LANES, rows), BF16),
            pltpu.VMEM((LANES, embed), BF16),
            pltpu.VMEM((8, lookups), I32),
            pltpu.VMEM((2, LANES, lookups), BF16),
            block,
            block,
            block,
            block,
            pltpu.VMEM((shards * SLOT_ROWS, bags), BF16),
            pltpu.VMEM((shards * SLOT_ROWS, bags), BF16),
            pltpu.VMEM((wide, rows), F32),
            pltpu.VMEM((LANES, bags), F32),
            pltpu.VMEM((replicas, tall, broad), BF16),
            pltpu.VMEM((replicas, tall, broad), BF16),
            pltpu.VMEM((tall, broad), BF16),
            pltpu.VMEM((replicas, tall, broad), BF16),
            pltpu.VMEM((holders, 8 * per, LANES), F32),
            pltpu.VMEM((shards, 8 * per, LANES), F32),
            pltpu.VMEM((8 * per, LANES), F32),
            pltpu.VMEM((replicas, 8 * per, LANES), F32),
            pltpu.VMEM((8 * per, LANES), F32),
            pltpu.VMEM((holders, 8 * per, LANES), F32),
            pltpu.SemaphoreType.DMA((11,)),
            pltpu.SemaphoreType.DMA((7,)),
            pltpu.SemaphoreType.DMA((GROUPS,)),
            pltpu.SemaphoreType.DMA((GROUPS,)),
            pltpu.SemaphoreType.DMA((5,)),
        ],
        compiler_params=pltpu.CompilerParams(
            collective_id=0, has_side_effects=True, vmem_limit_bytes=VMEM
        ),
    )(
        table_a.T,
        table_b.T,
        proj_a,
        proj_b,
        owner_a.reshape(line),
        row_a.reshape(line),
        bag_a,
        owner_b.reshape(line),
        row_b.reshape(line),
        bag_b,
        d_pooled,
    )
    pooled, grad_a, grad_b, proj_grad_a, proj_grad_b = pl.pallas_call(
        finish,
        out_shape=(
            jax.ShapeDtypeStruct((bags, embed), BF16),
            jax.ShapeDtypeStruct((wide_a, rows), F32),
            jax.ShapeDtypeStruct((wide - wide_a, rows), F32),
            jax.ShapeDtypeStruct((wide_a, embed), F32),
            jax.ShapeDtypeStruct((wide - wide_a, embed), F32),
        ),
        in_specs=[pl.BlockSpec(memory_space=pltpu.VMEM)] * 3,
        out_specs=(pl.BlockSpec(memory_space=pltpu.VMEM),) * 5,
        compiler_params=pltpu.CompilerParams(vmem_limit_bytes=VMEM),
    )(pooled, grads, grad_proj)
    return (pooled, grad_a.T, grad_b.T, proj_grad_a, proj_grad_b)


def solution(mesh):
    split = ("shard", "rep")
    tier = (P(split, None), P(split), P(split, None))
    in_specs = (P("shard", None), P("shard", None), P(), P(), *tier, *tier, P(split, None))
    out_specs = (P(split, None), P("shard", None), P("shard", None), P(), P())
    return jax.shard_map(body, mesh=mesh, in_specs=in_specs, out_specs=out_specs, check_vma=False)
```

```python
import functools

import jax
import jax.numpy as jnp
from jax import lax
from jax.experimental import pallas as pl
from jax.experimental.pallas import tpu as pltpu
from jax.sharding import PartitionSpec as P

F32, BF16, I32 = jnp.float32, jnp.bfloat16, jnp.int32
LANES = 128
TILE = 16
SLOT_ROWS = 24
GROUPS = 8
DIGIT = 5
VMEM = 64 * 1024 * 1024


def dot(left, right, dims=((1,), (0,))):
    return lax.dot_general(left, right, (dims, ((), ())), preferred_element_type=F32)


def iota(shape, dim):
    return lax.broadcasted_iota(I32, shape, dim)


def onehot(hit):
    return jnp.where(hit, 1.0, 0.0).astype(BF16)


def wait_bytes(ref, sem):
    pltpu.make_async_copy(ref, ref, sem).wait()


def digits(row, first, shape):
    at = iota(shape, 0)
    high, low = lax.shift_right_logical(row, DIGIT), jnp.bitwise_and(row, (1 << DIGIT) - 1)
    return jnp.where(at == first, high, jnp.where(at == first + 1, low, 0))


def column(block, lane):
    at = iota((1, LANES), 1)
    weight = jnp.where(at == lane, float(1 << DIGIT), jnp.where(at == lane + 1, 1.0, 0.0))
    return jnp.sum(block * weight, axis=1, keepdims=True).astype(I32)


def order(step, start, count):
    odd = step % 2
    return (start + count // 2 + (1 - odd) * (step // 2) - odd * ((step + 1) // 2) + count) % count


def kernel(
    shards,
    replicas,
    tab_a, tab_b, proj_a, proj_b, owner_a_in, row_a_in, bag_a_in, owner_b_in, row_b_in, bag_b_in, d_pooled_in,
    pooled_to, grads_to, proj_out,
    owner_a, row_a, bag_a, owner_b, row_b, bag_b, d_pooled,
    tabs, proj, slot, give, sent, came, found, back, bags_a, bags_b, grads, looked,
    piece, piece_in, share, share_in, part, part_in, tile, tile_in, done, done_in,
    pooled_out, grads_out, out_sems, in_sems, send_sems, came_sems, back_sems, recv_sems,
):
    me, rep = lax.axis_index("shard"), lax.axis_index("rep")
    lookups, rows, bags = owner_a.shape[1], tab_a.shape[1], d_pooled.shape[0]
    wide_a, wide_b = tab_a.shape[0], tab_b.shape[0]
    wide = wide_a + wide_b
    per_group = shards // GROUPS
    slots = per_group * SLOT_ROWS
    my_group = me // per_group
    holders, per = part.shape[0], part.shape[1] // TILE
    stride = shards // holders

    loads = [
        pltpu.make_async_copy(source, target, in_sems.at[k])
        for k, (source, target) in enumerate(
            (
                (owner_a_in, owner_a),
                (owner_b_in, owner_b),
                (bag_a_in, bag_a),
                (bag_b_in, bag_b),
                (row_a_in, row_a),
                (row_b_in, row_b),
                (proj_a, proj.at[0:wide_a]),
                (proj_b, proj.at[wide_a:wide]),
                (d_pooled_in, d_pooled),
                (tab_a, tabs.at[0, 0:wide_a]),
                (tab_b, tabs.at[1, wide_a:wide]),
            )
        )
    ]
    for load in loads:
        load.start()
    barrier = pltpu.get_barrier_semaphore()

    def each_rep(visit):
        def one(step, carry):
            visit(order(step, rep, replicas))
            return carry

        lax.fori_loop(0, replicas - 1, one, 0)

    def each_shard(visit):
        def group_of(step, carry):
            first = order(step, my_group, GROUPS) * per_group

            def one(i, inner):
                visit(first + i)
                return inner

            return lax.fori_loop(0, per_group, one, carry)

        lax.fori_loop(0, GROUPS - 1, group_of, 0)

        def beside(i, carry):
            visit(my_group * per_group + (me + i) % per_group)
            return carry

        lax.fori_loop(1, per_group, beside, 0)

    def greet(*target):
        pl.semaphore_signal(barrier, inc=1, device_id=target, device_id_type=pl.DeviceIdType.MESH)

    each_rep(lambda target: greet(me, target))
    each_shard(lambda target: greet(target, rep))

    proj[wide:, :] = jnp.zeros((LANES - wide, proj.shape[1]), BF16)
    tabs[0, wide_a:, :] = jnp.zeros((LANES - wide_a, rows), BF16)
    tabs[1, 0:wide_a, :] = jnp.zeros((wide_a, rows), BF16)
    tabs[1, wide:, :] = jnp.zeros((LANES - wide, rows), BF16)
    give[0, wide_a:wide, :] = jnp.zeros((wide - wide_a, lookups), BF16)
    give[1, 0:wide_a, :] = jnp.zeros((wide_a, lookups), BF16)
    for load in loads[:9]:
        load.wait()

    row_grad = dot(proj[...], d_pooled[...], ((1,), (1,))).astype(BF16)
    chunk = min(256, lookups)
    before = onehot(iota((chunk, chunk), 0) < iota((chunk, chunk), 1))
    carried = jnp.zeros((2 * shards, 1), F32)
    for first in range(0, lookups, chunk):
        cut = slice(first, first + chunk)
        named_a = owner_a[:, cut] == iota((shards, chunk), 0)
        named_b = owner_b[:, cut] == iota((shards, chunk), 0)
        named = jnp.concatenate([jnp.where(named_a, 1.0, 0.0), jnp.where(named_b, 1.0, 0.0)])
        earlier = dot(named.astype(BF16), before) + carried
        carried = carried + jnp.sum(named, axis=1, keepdims=True)
        earlier = earlier * named
        place_a = jnp.sum(earlier[:shards], axis=0, keepdims=True).astype(I32)
        place_b = jnp.sum(earlier[shards:], axis=0, keepdims=True).astype(I32)
        slot[0:1, cut] = owner_a[:, cut] * SLOT_ROWS + place_a
        slot[1:2, cut] = owner_b[:, cut] * SLOT_ROWS + place_b
        in_bag = onehot(bag_a[:, cut] == iota((bags, chunk), 0))
        give[0, 0:wide_a, cut] = dot(row_grad[0:wide_a], in_bag).astype(BF16)
        in_bag = onehot(bag_b[:, cut] == iota((bags, chunk), 0))
        give[1, wide_a:wide, cut] = dot(row_grad[wide_a:wide], in_bag).astype(BF16)
        tail = (LANES - wide, chunk)
        give[0, wide:, cut] = (digits(row_a[:, cut], 0, tail) + digits(bag_a[:, cut] + 1, 2, tail)).astype(F32).astype(BF16)
        give[1, wide:, cut] = (digits(row_b[:, cut], 4, tail) + digits(bag_b[:, cut] + 1, 6, tail)).astype(F32).astype(BF16)

    pl.semaphore_wait(barrier, shards + replicas - 2)

    def to_shard(block, there, target, send_sem, recv_sem):
        pltpu.make_async_remote_copy(
            src_ref=block,
            dst_ref=there,
            send_sem=send_sem,
            recv_sem=recv_sem,
            device_id=(target, rep),
            device_id_type=pl.DeviceIdType.MESH,
        ).start()

    def to_rep(block, there, target, send_sem, recv_sem):
        pltpu.make_async_remote_copy(
            src_ref=block,
            dst_ref=there,
            send_sem=send_sem,
            recv_sem=recv_sem,
            device_id=(me, target),
            device_id_type=pl.DeviceIdType.MESH,
        ).start()

    def send_group(group, source, landing, send_sem, recv_sem):
        def one(i, carry):
            target = group * per_group + i

            @pl.when(target != me)
            def _():
                to_shard(source.at[target], landing.at[me], target, send_sem, recv_sem)

            @pl.when(target == me)
            def _():
                pltpu.make_async_copy(source.at[target], landing.at[me], recv_sem).start()

            return carry

        lax.fori_loop(0, per_group, one, 0)

    def ask(step, carry):
        group = order(step, my_group, GROUPS)
        at = iota((slots, lookups), 0) + group * slots
        block = dot(onehot(slot[0:1, :] == at), give[0], ((1,), (1,)))
        block += dot(onehot(slot[1:2, :] == at), give[1], ((1,), (1,)))
        sent[pl.ds(group * per_group, per_group)] = block.reshape(per_group, SLOT_ROWS, LANES).astype(BF16)
        send_group(group, sent, came, send_sems.at[0], came_sems.at[my_group])
        return carry

    lax.fori_loop(0, GROUPS, ask, 0)

    grads[...] = jnp.zeros_like(grads)
    looked[...] = jnp.zeros_like(looked)

    for load in loads[9:]:
        load.wait()

    def answer(step, carry):
        group = order(step, my_group, GROUPS)
        mine = pl.ds(group * per_group, per_group)
        wait_bytes(came.at[mine], came_sems.at[group])
        block = came[mine].astype(F32).reshape(slots, LANES)
        at = iota((slots, rows), 1)
        hot_a = onehot(column(block, wide) == at)
        hot_b = onehot(column(block, wide + 4) == at)
        gathered = dot(hot_a, tabs[0], ((1,), (1,))) + dot(hot_b, tabs[1], ((1,), (1,)))
        found[mine] = gathered.reshape(per_group, SLOT_ROWS, LANES).astype(BF16)
        send_group(group, found, back, send_sems.at[1], back_sems.at[my_group])
        turned = block.T.astype(BF16)
        grads[0:wide_a, :] += dot(turned[0:wide_a], hot_a)
        grads[wide_a:wide, :] += dot(turned[wide_a:wide], hot_b)
        return carry

    lax.fori_loop(0, GROUPS, answer, 0)

    tall, broad = piece.shape[1], piece.shape[2]
    across = rows // broad
    for k in range(replicas):
        high, left = (k // across) * tall, (k % across) * broad
        piece[k] = grads[high : high + tall, left : left + broad].astype(BF16)
    piece_in[rep] = piece[rep]

    each_rep(lambda target: to_rep(piece.at[target], piece_in.at[rep], target, send_sems.at[2], recv_sems.at[0]))

    def mark(group, carry):
        block = sent[pl.ds(group * per_group, per_group)].astype(F32).reshape(slots, LANES)
        at = iota((slots, bags), 1) + 1
        bags_a[pl.ds(group * slots, slots), :] = onehot(column(block, wide + 2) == at)
        bags_b[pl.ds(group * slots, slots), :] = onehot(column(block, wide + 6) == at)
        return carry

    lax.fori_loop(0, GROUPS, mark, 0)

    def pool(step, carry):
        group = order(step, my_group, GROUPS)
        mine = pl.ds(group * per_group, per_group)
        wait_bytes(back.at[mine], back_sems.at[group])
        turned = back[mine].astype(F32).reshape(slots, LANES).T.astype(BF16)
        here = pl.ds(group * slots, slots)
        looked[0:wide_a, :] += dot(turned[0:wide_a], bags_a[here, :])
        looked[wide_a:wide, :] += dot(turned[wide_a:wide], bags_b[here, :])
        return carry

    lax.fori_loop(0, GROUPS, pool, 0)

    high = looked[...].astype(BF16)
    low = (looked[...] - high.astype(F32)).astype(BF16)
    partial = dot(high, d_pooled[...]) + dot(low, d_pooled[...])
    embed = partial.shape[1]
    halves = embed // LANES
    for k in range(holders * per):
        top, left = (k // halves) * TILE, (k % halves) * LANES
        first = (k % per) * TILE
        part[k // per, first : first + TILE, :] = partial[top : top + TILE, left : left + LANES].astype(BF16)
    index = me // stride
    holding = jnp.logical_and(me == index * stride, index < holders)

    def hand(step, carry):
        target = (index + step) % holders

        @pl.when(target * stride != me)
        def _():
            to_shard(part.at[target], part_in.at[me], target * stride, send_sems.at[4], recv_sems.at[2])

        return carry

    lax.fori_loop(0, holders, hand, 0)

    @pl.when(holding)
    def _():
        part_in[me] = part[index]
        wait_bytes(part_in.at[pl.ds(0, shards - 1)], recv_sems.at[2])
        tile[...] = jnp.sum(part_in[...].astype(F32), axis=0).astype(BF16)
        tile_in[rep] = tile[...]
        each_rep(lambda target: to_rep(tile, tile_in.at[rep], target, send_sems.at[5], recv_sems.at[3]))

    wait_bytes(piece_in.at[pl.ds(0, replicas - 1)], recv_sems.at[0])
    share[...] = jnp.sum(piece_in[...].astype(F32), axis=0).astype(BF16)
    share_in[rep] = share[...]

    each_rep(lambda target: to_rep(share, share_in.at[rep], target, send_sems.at[3], recv_sems.at[1]))

    @pl.when(holding)
    def _():
        wait_bytes(tile_in.at[pl.ds(0, replicas - 1)], recv_sems.at[3])
        scale = 1.0 / (float(lookups * shards * replicas) ** 0.5)
        done[...] = (jnp.sum(tile_in[...].astype(F32), axis=0) * scale).astype(BF16)
        done_in[index] = done[...]
        each_shard(lambda target: to_shard(done, done_in.at[index], target, send_sems.at[6], recv_sems.at[4]))

    turned = looked[...].T
    high = turned.astype(BF16)
    low = (turned - high.astype(F32)).astype(BF16)
    pooled_out[...] = (dot(high, proj[...]) + dot(low, proj[...])).astype(BF16)
    store_pooled = pltpu.make_async_copy(pooled_out, pooled_to, out_sems.at[0])
    store_pooled.start()

    wait_bytes(share_in.at[pl.ds(0, replicas - 1)], recv_sems.at[1])
    for k in range(replicas):
        top, left = (k // across) * tall, (k % across) * broad
        grads_out[top : top + tall, left : left + broad] = share_in[k]
    store_grads = pltpu.make_async_copy(grads_out, grads_to, out_sems.at[1])
    store_grads.start()

    @pl.when(holding)
    def _():
        wait_bytes(done_in.at[pl.ds(0, holders - 1)], recv_sems.at[4])

    @pl.when(jnp.logical_not(holding))
    def _():
        wait_bytes(done_in, recv_sems.at[4])

    for k in range(holders * per):
        top, left = (k // halves) * TILE, (k % halves) * LANES
        first = (k % per) * TILE
        proj_out[top : top + TILE, left : left + LANES] = done_in[k // per, first : first + TILE, :].astype(F32)

    store_pooled.wait()
    store_grads.wait()
    wait_bytes(sent.at[pl.ds(0, shards - 1)], send_sems.at[0])
    wait_bytes(found.at[pl.ds(0, shards - 1)], send_sems.at[1])
    wait_bytes(piece.at[pl.ds(0, replicas - 1)], send_sems.at[2])
    wait_bytes(share_in.at[pl.ds(0, replicas - 1)], send_sems.at[3])

    @pl.when(holding)
    def _():
        wait_bytes(part.at[pl.ds(0, holders - 1)], send_sems.at[4])
        wait_bytes(tile_in.at[pl.ds(0, replicas - 1)], send_sems.at[5])
        wait_bytes(part_in.at[pl.ds(0, shards - 1)], send_sems.at[6])

    @pl.when(jnp.logical_not(holding))
    def _():
        wait_bytes(part, send_sems.at[4])


def finish(pooled, grads, grad_proj, pooled_out, grad_a, grad_b, proj_a, proj_b):
    wide_a = grad_a.shape[0]
    pooled_out[...] = pooled[...]
    grad_a[...] = grads[0:wide_a, :].astype(F32)
    grad_b[...] = grads[wide_a:, :].astype(F32)
    proj_a[...] = grad_proj[0:wide_a, :]
    proj_b[...] = grad_proj[wide_a:, :]


def body(table_a, table_b, proj_a, proj_b, owner_a, row_a, bag_a, owner_b, row_b, bag_b, d_pooled):
    shards, replicas = lax.axis_size("shard"), lax.axis_size("rep")
    lookups = row_a.shape[0]
    rows, wide_a = table_a.shape
    wide = wide_a + table_b.shape[1]
    bags, embed = d_pooled.shape
    tiles = wide * embed // (TILE * LANES)
    holders = max(h for h in range(1, min(tiles, shards) + 1) if tiles % h == 0)
    per = tiles // holders
    tall, broad = wide // 2, 2 * rows // replicas
    block = pltpu.VMEM((shards, SLOT_ROWS, LANES), BF16)
    line = (1, lookups)
    pooled, grads, grad_proj = pl.pallas_call(
        functools.partial(kernel, shards, replicas),
        out_shape=(
            jax.ShapeDtypeStruct((bags, embed), BF16),
            jax.ShapeDtypeStruct((wide, rows), BF16),
            jax.ShapeDtypeStruct((wide, embed), F32),
        ),
        in_specs=[pl.BlockSpec(memory_space=pltpu.HBM)] * 11,
        out_specs=(
            pl.BlockSpec(memory_space=pltpu.HBM),
            pl.BlockSpec(memory_space=pltpu.HBM),
            pl.BlockSpec(memory_space=pltpu.VMEM),
        ),
        scratch_shapes=[
            pltpu.VMEM(line, I32),
            pltpu.VMEM(line, I32),
            pltpu.VMEM(line, I32),
            pltpu.VMEM(line, I32),
            pltpu.VMEM(line, I32),
            pltpu.VMEM(line, I32),
            pltpu.VMEM((bags, embed), BF16),
            pltpu.VMEM((2, LANES, rows), BF16),
            pltpu.VMEM((LANES, embed), BF16),
            pltpu.VMEM((8, lookups), I32),
            pltpu.VMEM((2, LANES, lookups), BF16),
            block,
            block,
            block,
            block,
            pltpu.VMEM((shards * SLOT_ROWS, bags), BF16),
            pltpu.VMEM((shards * SLOT_ROWS, bags), BF16),
            pltpu.VMEM((wide, rows), F32),
            pltpu.VMEM((LANES, bags), F32),
            pltpu.VMEM((replicas, tall, broad), BF16),
            pltpu.VMEM((replicas, tall, broad), BF16),
            pltpu.VMEM((tall, broad), BF16),
            pltpu.VMEM((replicas, tall, broad), BF16),
            pltpu.VMEM((holders, TILE * per, LANES), BF16),
            pltpu.VMEM((shards, TILE * per, LANES), BF16),
            pltpu.VMEM((TILE * per, LANES), BF16),
            pltpu.VMEM((replicas, TILE * per, LANES), BF16),
            pltpu.VMEM((TILE * per, LANES), BF16),
            pltpu.VMEM((holders, TILE * per, LANES), BF16),
            pltpu.VMEM((bags, embed), BF16),
            pltpu.VMEM((wide, rows), BF16),
            pltpu.SemaphoreType.DMA((2,)),
            pltpu.SemaphoreType.DMA((11,)),
            pltpu.SemaphoreType.DMA((7,)),
            pltpu.SemaphoreType.DMA((GROUPS,)),
            pltpu.SemaphoreType.DMA((GROUPS,)),
            pltpu.SemaphoreType.DMA((5,)),
        ],
        compiler_params=pltpu.CompilerParams(
            collective_id=0, has_side_effects=True, vmem_limit_bytes=VMEM
        ),
    )(
        table_a.T,
        table_b.T,
        proj_a,
        proj_b,
        owner_a.reshape(line),
        row_a.reshape(line),
        bag_a,
        owner_b.reshape(line),
        row_b.reshape(line),
        bag_b,
        d_pooled,
    )
    pooled, grad_a, grad_b, proj_grad_a, proj_grad_b = pl.pallas_call(
        finish,
        out_shape=(
            jax.ShapeDtypeStruct((bags, embed), BF16),
            jax.ShapeDtypeStruct((wide_a, rows), F32),
            jax.ShapeDtypeStruct((wide - wide_a, rows), F32),
            jax.ShapeDtypeStruct((wide_a, embed), F32),
            jax.ShapeDtypeStruct((wide - wide_a, embed), F32),
        ),
        in_specs=[pl.BlockSpec(memory_space=pltpu.VMEM)] * 3,
        out_specs=(pl.BlockSpec(memory_space=pltpu.VMEM),) * 5,
        compiler_params=pltpu.CompilerParams(vmem_limit_bytes=VMEM),
    )(pooled, grads, grad_proj)
    return (pooled, grad_a.T, grad_b.T, proj_grad_a, proj_grad_b)


def solution(mesh):
    split = ("shard", "rep")
    tier = (P(split, None), P(split), P(split, None))
    in_specs = (P("shard", None), P("shard", None), P(), P(), *tier, *tier, P(split, None))
    out_specs = (P(split, None), P("shard", None), P("shard", None), P(), P())
    return jax.shard_map(body, mesh=mesh, in_specs=in_specs, out_specs=out_specs, check_vma=False)
```

```python
import functools

import jax
import jax.numpy as jnp
from jax import lax
from jax.experimental import pallas as pl
from jax.experimental.pallas import tpu as pltpu
from jax.sharding import PartitionSpec as P

F32, BF16, I32 = jnp.float32, jnp.bfloat16, jnp.int32
LANES = 128
TILE = 16
SLOT_ROWS = 24
GROUPS = 8
DIGIT = 5
LIMIT, SMALL = 48 * 1024 * 1024, 16 * 1024 * 1024


def dot(left, right, dims=((1,), (0,))):
    return lax.dot_general(left, right, (dims, ((), ())), preferred_element_type=F32)


def iota(shape, dim):
    return lax.broadcasted_iota(I32, shape, dim)


def onehot(hit):
    return jnp.where(hit, 1.0, 0.0).astype(BF16)


def wait_bytes(ref, sem):
    pltpu.make_async_copy(ref, ref, sem).wait()


def digits(row, first, shape):
    at = iota(shape, 0)
    high, low = lax.shift_right_logical(row, DIGIT), jnp.bitwise_and(row, (1 << DIGIT) - 1)
    return jnp.where(at == first, high, jnp.where(at == first + 1, low, 0))


def column(block, lane):
    at = iota((1, LANES), 1)
    weight = jnp.where(at == lane, float(1 << DIGIT), jnp.where(at == lane + 1, 1.0, 0.0))
    return jnp.sum(block * weight, axis=1, keepdims=True).astype(I32)


def order(step, start, count):
    odd = step % 2
    return (start + count // 2 + (1 - odd) * (step // 2) - odd * ((step + 1) // 2) + count) % count


def kernel(
    shards,
    replicas,
    tab_a, tab_b, proj_a, proj_b, owner_a_in, row_a_in, bag_a_in, owner_b_in, row_b_in, bag_b_in, d_pooled_in,
    pooled_out, grads_out, proj_out,
    owner_a, row_a, bag_a, owner_b, row_b, bag_b, d_pooled,
    tabs, proj, slot, give, sent, came, found, back, bags_a, bags_b, grads, looked,
    piece, piece_in, share, share_in, part, part_in, tile, tile_in, done, done_in,
    in_sems, send_sems, came_sems, back_sems, recv_sems,
):
    me, rep = lax.axis_index("shard"), lax.axis_index("rep")
    lookups, rows, bags = owner_a.shape[1], tab_a.shape[1], d_pooled.shape[0]
    wide_a, wide_b = tab_a.shape[0], tab_b.shape[0]
    wide = wide_a + wide_b
    per_group = shards // GROUPS
    slots = per_group * SLOT_ROWS
    my_group = me // per_group
    holders, per = part.shape[0], part.shape[1] // TILE
    stride = shards // holders

    loads = [
        pltpu.make_async_copy(source, target, in_sems.at[k])
        for k, (source, target) in enumerate(
            (
                (owner_a_in, owner_a),
                (owner_b_in, owner_b),
                (bag_a_in, bag_a),
                (bag_b_in, bag_b),
                (row_a_in, row_a),
                (row_b_in, row_b),
                (proj_a, proj.at[0:wide_a]),
                (proj_b, proj.at[wide_a:wide]),
                (d_pooled_in, d_pooled),
                (tab_a, tabs.at[0, 0:wide_a]),
                (tab_b, tabs.at[1, wide_a:wide]),
            )
        )
    ]
    for load in loads:
        load.start()
    barrier = pltpu.get_barrier_semaphore()

    def each_rep(visit):
        def one(step, carry):
            visit(order(step, rep, replicas))
            return carry

        lax.fori_loop(0, replicas - 1, one, 0)

    def each_shard(visit):
        def group_of(step, carry):
            first = order(step, my_group, GROUPS) * per_group

            def one(i, inner):
                visit(first + i)
                return inner

            return lax.fori_loop(0, per_group, one, carry)

        lax.fori_loop(0, GROUPS - 1, group_of, 0)

        def beside(i, carry):
            visit(my_group * per_group + (me + i) % per_group)
            return carry

        lax.fori_loop(1, per_group, beside, 0)

    def greet(*target):
        pl.semaphore_signal(barrier, inc=1, device_id=target, device_id_type=pl.DeviceIdType.MESH)

    each_rep(lambda target: greet(me, target))
    each_shard(lambda target: greet(target, rep))

    proj[wide:, :] = jnp.zeros((LANES - wide, proj.shape[1]), BF16)
    tabs[0, wide_a:, :] = jnp.zeros((LANES - wide_a, rows), BF16)
    tabs[1, 0:wide_a, :] = jnp.zeros((wide_a, rows), BF16)
    tabs[1, wide:, :] = jnp.zeros((LANES - wide, rows), BF16)
    give[0, wide_a:wide, :] = jnp.zeros((wide - wide_a, lookups), BF16)
    give[1, 0:wide_a, :] = jnp.zeros((wide_a, lookups), BF16)
    for load in loads[:9]:
        load.wait()

    row_grad = dot(proj[...], d_pooled[...], ((1,), (1,))).astype(BF16)
    chunk = min(256, lookups)
    before = onehot(iota((chunk, chunk), 0) < iota((chunk, chunk), 1))
    carried = jnp.zeros((2 * shards, 1), F32)
    for first in range(0, lookups, chunk):
        cut = slice(first, first + chunk)
        named_a = owner_a[:, cut] == iota((shards, chunk), 0)
        named_b = owner_b[:, cut] == iota((shards, chunk), 0)
        named = jnp.concatenate([jnp.where(named_a, 1.0, 0.0), jnp.where(named_b, 1.0, 0.0)])
        earlier = dot(named.astype(BF16), before) + carried
        carried = carried + jnp.sum(named, axis=1, keepdims=True)
        earlier = earlier * named
        place_a = jnp.sum(earlier[:shards], axis=0, keepdims=True).astype(I32)
        place_b = jnp.sum(earlier[shards:], axis=0, keepdims=True).astype(I32)
        slot[0:1, cut] = owner_a[:, cut] * SLOT_ROWS + place_a
        slot[1:2, cut] = owner_b[:, cut] * SLOT_ROWS + place_b
        in_bag = onehot(bag_a[:, cut] == iota((bags, chunk), 0))
        give[0, 0:wide_a, cut] = dot(row_grad[0:wide_a], in_bag).astype(BF16)
        in_bag = onehot(bag_b[:, cut] == iota((bags, chunk), 0))
        give[1, wide_a:wide, cut] = dot(row_grad[wide_a:wide], in_bag).astype(BF16)
        tail = (LANES - wide, chunk)
        give[0, wide:, cut] = (digits(row_a[:, cut], 0, tail) + digits(bag_a[:, cut] + 1, 2, tail)).astype(F32).astype(BF16)
        give[1, wide:, cut] = (digits(row_b[:, cut], 4, tail) + digits(bag_b[:, cut] + 1, 6, tail)).astype(F32).astype(BF16)

    pl.semaphore_wait(barrier, shards + replicas - 2)

    def to_shard(block, there, target, send_sem, recv_sem):
        pltpu.make_async_remote_copy(
            src_ref=block,
            dst_ref=there,
            send_sem=send_sem,
            recv_sem=recv_sem,
            device_id=(target, rep),
            device_id_type=pl.DeviceIdType.MESH,
        ).start()

    def to_rep(block, there, target, send_sem, recv_sem):
        pltpu.make_async_remote_copy(
            src_ref=block,
            dst_ref=there,
            send_sem=send_sem,
            recv_sem=recv_sem,
            device_id=(me, target),
            device_id_type=pl.DeviceIdType.MESH,
        ).start()

    def send_group(group, source, landing, send_sem, recv_sem):
        def one(i, carry):
            target = group * per_group + i

            @pl.when(target != me)
            def _():
                to_shard(source.at[target], landing.at[me], target, send_sem, recv_sem)

            @pl.when(target == me)
            def _():
                pltpu.make_async_copy(source.at[target], landing.at[me], recv_sem).start()

            return carry

        lax.fori_loop(0, per_group, one, 0)

    def ask(step, carry):
        group = order(step, my_group, GROUPS)
        at = iota((slots, lookups), 0) + group * slots
        block = dot(onehot(slot[0:1, :] == at), give[0], ((1,), (1,)))
        block += dot(onehot(slot[1:2, :] == at), give[1], ((1,), (1,)))
        sent[pl.ds(group * per_group, per_group)] = block.reshape(per_group, SLOT_ROWS, LANES).astype(BF16)
        send_group(group, sent, came, send_sems.at[0], came_sems.at[my_group])
        return carry

    lax.fori_loop(0, GROUPS, ask, 0)

    grads[...] = jnp.zeros_like(grads)
    looked[...] = jnp.zeros_like(looked)

    for load in loads[9:]:
        load.wait()

    def answer(step, carry):
        group = order(step, my_group, GROUPS)
        mine = pl.ds(group * per_group, per_group)
        wait_bytes(came.at[mine], came_sems.at[group])
        block = came[mine].astype(F32).reshape(slots, LANES)
        at = iota((slots, rows), 1)
        hot_a = onehot(column(block, wide) == at)
        hot_b = onehot(column(block, wide + 4) == at)
        gathered = dot(hot_a, tabs[0], ((1,), (1,))) + dot(hot_b, tabs[1], ((1,), (1,)))
        found[mine] = gathered.reshape(per_group, SLOT_ROWS, LANES).astype(BF16)
        send_group(group, found, back, send_sems.at[1], back_sems.at[my_group])
        turned = block.T.astype(BF16)
        grads[0:wide_a, :] += dot(turned[0:wide_a], hot_a)
        grads[wide_a:wide, :] += dot(turned[wide_a:wide], hot_b)
        return carry

    lax.fori_loop(0, GROUPS, answer, 0)

    tall, broad = piece.shape[1], piece.shape[2]
    across = rows // broad
    for k in range(replicas):
        high, left = (k // across) * tall, (k % across) * broad
        piece[k] = grads[high : high + tall, left : left + broad].astype(BF16)
    piece_in[rep] = piece[rep]

    each_rep(lambda target: to_rep(piece.at[target], piece_in.at[rep], target, send_sems.at[2], recv_sems.at[0]))

    def mark(group, carry):
        block = sent[pl.ds(group * per_group, per_group)].astype(F32).reshape(slots, LANES)
        at = iota((slots, bags), 1) + 1
        bags_a[pl.ds(group * slots, slots), :] = onehot(column(block, wide + 2) == at)
        bags_b[pl.ds(group * slots, slots), :] = onehot(column(block, wide + 6) == at)
        return carry

    lax.fori_loop(0, GROUPS, mark, 0)

    def pool(step, carry):
        group = order(step, my_group, GROUPS)
        mine = pl.ds(group * per_group, per_group)
        wait_bytes(back.at[mine], back_sems.at[group])
        turned = back[mine].astype(F32).reshape(slots, LANES).T.astype(BF16)
        here = pl.ds(group * slots, slots)
        looked[0:wide_a, :] += dot(turned[0:wide_a], bags_a[here, :])
        looked[wide_a:wide, :] += dot(turned[wide_a:wide], bags_b[here, :])
        return carry

    lax.fori_loop(0, GROUPS, pool, 0)

    high = looked[...].astype(BF16)
    low = (looked[...] - high.astype(F32)).astype(BF16)
    partial = dot(high, d_pooled[...]) + dot(low, d_pooled[...])
    embed = partial.shape[1]
    halves = embed // LANES
    for k in range(holders * per):
        top, left = (k // halves) * TILE, (k % halves) * LANES
        first = (k % per) * TILE
        part[k // per, first : first + TILE, :] = partial[top : top + TILE, left : left + LANES].astype(BF16)
    index = me // stride
    holding = jnp.logical_and(me == index * stride, index < holders)

    def hand(step, carry):
        target = (index + step) % holders

        @pl.when(target * stride != me)
        def _():
            to_shard(part.at[target], part_in.at[me], target * stride, send_sems.at[4], recv_sems.at[2])

        return carry

    lax.fori_loop(0, holders, hand, 0)

    @pl.when(holding)
    def _():
        part_in[me] = part[index]
        wait_bytes(part_in.at[pl.ds(0, shards - 1)], recv_sems.at[2])
        tile[...] = jnp.sum(part_in[...].astype(F32), axis=0).astype(BF16)
        tile_in[rep] = tile[...]
        each_rep(lambda target: to_rep(tile, tile_in.at[rep], target, send_sems.at[5], recv_sems.at[3]))

    wait_bytes(piece_in.at[pl.ds(0, replicas - 1)], recv_sems.at[0])
    share[...] = jnp.sum(piece_in[...].astype(F32), axis=0).astype(BF16)
    share_in[rep] = share[...]

    each_rep(lambda target: to_rep(share, share_in.at[rep], target, send_sems.at[3], recv_sems.at[1]))

    @pl.when(holding)
    def _():
        wait_bytes(tile_in.at[pl.ds(0, replicas - 1)], recv_sems.at[3])
        scale = 1.0 / (float(lookups * shards * replicas) ** 0.5)
        done[...] = (jnp.sum(tile_in[...].astype(F32), axis=0) * scale).astype(BF16)
        done_in[index] = done[...]
        each_shard(lambda target: to_shard(done, done_in.at[index], target, send_sems.at[6], recv_sems.at[4]))

    turned = looked[...].T
    high = turned.astype(BF16)
    low = (turned - high.astype(F32)).astype(BF16)
    pooled_out[...] = (dot(high, proj[...]) + dot(low, proj[...])).astype(BF16)

    wait_bytes(share_in.at[pl.ds(0, replicas - 1)], recv_sems.at[1])
    for k in range(replicas):
        top, left = (k // across) * tall, (k % across) * broad
        grads_out[top : top + tall, left : left + broad] = share_in[k]

    @pl.when(holding)
    def _():
        wait_bytes(done_in.at[pl.ds(0, holders - 1)], recv_sems.at[4])

    @pl.when(jnp.logical_not(holding))
    def _():
        wait_bytes(done_in, recv_sems.at[4])

    for k in range(holders * per):
        top, left = (k // halves) * TILE, (k % halves) * LANES
        first = (k % per) * TILE
        proj_out[top : top + TILE, left : left + LANES] = done_in[k // per, first : first + TILE, :].astype(F32)

    wait_bytes(sent.at[pl.ds(0, shards - 1)], send_sems.at[0])
    wait_bytes(found.at[pl.ds(0, shards - 1)], send_sems.at[1])
    wait_bytes(piece.at[pl.ds(0, replicas - 1)], send_sems.at[2])
    wait_bytes(share_in.at[pl.ds(0, replicas - 1)], send_sems.at[3])

    @pl.when(holding)
    def _():
        wait_bytes(part.at[pl.ds(0, holders - 1)], send_sems.at[4])
        wait_bytes(tile_in.at[pl.ds(0, replicas - 1)], send_sems.at[5])
        wait_bytes(part_in.at[pl.ds(0, shards - 1)], send_sems.at[6])

    @pl.when(jnp.logical_not(holding))
    def _():
        wait_bytes(part, send_sems.at[4])


def finish(pooled, grads, grad_proj, pooled_out, grad_a, grad_b, proj_a, proj_b):
    wide_a = grad_a.shape[0]
    pooled_out[...] = pooled[...]
    grad_a[...] = grads[0:wide_a, :].astype(F32)
    grad_b[...] = grads[wide_a:, :].astype(F32)
    proj_a[...] = grad_proj[0:wide_a, :]
    proj_b[...] = grad_proj[wide_a:, :]


def body(table_a, table_b, proj_a, proj_b, owner_a, row_a, bag_a, owner_b, row_b, bag_b, d_pooled):
    shards, replicas = lax.axis_size("shard"), lax.axis_size("rep")
    lookups = row_a.shape[0]
    rows, wide_a = table_a.shape
    wide = wide_a + table_b.shape[1]
    bags, embed = d_pooled.shape
    tiles = wide * embed // (TILE * LANES)
    holders = max(h for h in range(1, min(tiles, shards) + 1) if tiles % h == 0)
    per = tiles // holders
    tall, broad = wide // 2, 2 * rows // replicas
    block = pltpu.VMEM((shards, SLOT_ROWS, LANES), BF16)
    line = (1, lookups)
    pooled, grads, grad_proj = pl.pallas_call(
        functools.partial(kernel, shards, replicas),
        out_shape=(
            jax.ShapeDtypeStruct((bags, embed), BF16),
            jax.ShapeDtypeStruct((wide, rows), BF16),
            jax.ShapeDtypeStruct((wide, embed), F32),
        ),
        in_specs=[pl.BlockSpec(memory_space=pltpu.HBM)] * 11,
        out_specs=(pl.BlockSpec(memory_space=pltpu.VMEM),) * 3,
        scratch_shapes=[
            pltpu.VMEM(line, I32),
            pltpu.VMEM(line, I32),
            pltpu.VMEM(line, I32),
            pltpu.VMEM(line, I32),
            pltpu.VMEM(line, I32),
            pltpu.VMEM(line, I32),
            pltpu.VMEM((bags, embed), BF16),
            pltpu.VMEM((2, LANES, rows), BF16),
            pltpu.VMEM((LANES, embed), BF16),
            pltpu.VMEM((8, lookups), I32),
            pltpu.VMEM((2, LANES, lookups), BF16),
            block,
            block,
            block,
            block,
            pltpu.VMEM((shards * SLOT_ROWS, bags), BF16),
            pltpu.VMEM((shards * SLOT_ROWS, bags), BF16),
            pltpu.VMEM((wide, rows), F32),
            pltpu.VMEM((LANES, bags), F32),
            pltpu.VMEM((replicas, tall, broad), BF16),
            pltpu.VMEM((replicas, tall, broad), BF16),
            pltpu.VMEM((tall, broad), BF16),
            pltpu.VMEM((replicas, tall, broad), BF16),
            pltpu.VMEM((holders, TILE * per, LANES), BF16),
            pltpu.VMEM((shards, TILE * per, LANES), BF16),
            pltpu.VMEM((TILE * per, LANES), BF16),
            pltpu.VMEM((replicas, TILE * per, LANES), BF16),
            pltpu.VMEM((TILE * per, LANES), BF16),
            pltpu.VMEM((holders, TILE * per, LANES), BF16),
            pltpu.SemaphoreType.DMA((11,)),
            pltpu.SemaphoreType.DMA((7,)),
            pltpu.SemaphoreType.DMA((GROUPS,)),
            pltpu.SemaphoreType.DMA((GROUPS,)),
            pltpu.SemaphoreType.DMA((5,)),
        ],
        compiler_params=pltpu.CompilerParams(
            collective_id=0, has_side_effects=True, vmem_limit_bytes=LIMIT
        ),
    )(
        *(
            pltpu.with_memory_space_constraint(x, pltpu.HBM)
            for x in (
                table_a.T,
                table_b.T,
                proj_a,
                proj_b,
                owner_a.reshape(line),
                row_a.reshape(line),
                bag_a,
                owner_b.reshape(line),
                row_b.reshape(line),
                bag_b,
                d_pooled,
            )
        )
    )
    pooled, grad_a, grad_b, proj_grad_a, proj_grad_b = pl.pallas_call(
        finish,
        out_shape=(
            jax.ShapeDtypeStruct((bags, embed), BF16),
            jax.ShapeDtypeStruct((wide_a, rows), F32),
            jax.ShapeDtypeStruct((wide - wide_a, rows), F32),
            jax.ShapeDtypeStruct((wide_a, embed), F32),
            jax.ShapeDtypeStruct((wide - wide_a, embed), F32),
        ),
        in_specs=[pl.BlockSpec(memory_space=pltpu.VMEM)] * 3,
        out_specs=(pl.BlockSpec(memory_space=pltpu.VMEM),) * 5,
        compiler_params=pltpu.CompilerParams(vmem_limit_bytes=SMALL),
    )(pooled, grads, grad_proj)
    return (pooled, grad_a.T, grad_b.T, proj_grad_a, proj_grad_b)


def solution(mesh):
    split = ("shard", "rep")
    tier = (P(split, None), P(split), P(split, None))
    in_specs = (P("shard", None), P("shard", None), P(), P(), *tier, *tier, P(split, None))
    out_specs = (P(split, None), P("shard", None), P("shard", None), P(), P())
    return jax.shard_map(body, mesh=mesh, in_specs=in_specs, out_specs=out_specs, check_vma=False)
```

```python
import functools

import jax
import jax.numpy as jnp
from jax import lax
from jax.experimental import pallas as pl
from jax.experimental.pallas import tpu as pltpu
from jax.sharding import PartitionSpec as P

F32, BF16, I32 = jnp.float32, jnp.bfloat16, jnp.int32
LANES = 128
TILE = 16
SLOT_ROWS = 24
GROUPS = 8
DIGIT = 5
LIMIT, SMALL = 48 * 1024 * 1024, 16 * 1024 * 1024


def dot(left, right, dims=((1,), (0,))):
    return lax.dot_general(left, right, (dims, ((), ())), preferred_element_type=F32)


def iota(shape, dim):
    return lax.broadcasted_iota(I32, shape, dim)


def onehot(hit):
    return jnp.where(hit, 1.0, 0.0).astype(BF16)


def wait_bytes(ref, sem):
    pltpu.make_async_copy(ref, ref, sem).wait()


def digits(row, first, shape):
    at = iota(shape, 0)
    high, low = lax.shift_right_logical(row, DIGIT), jnp.bitwise_and(row, (1 << DIGIT) - 1)
    return jnp.where(at == first, high, jnp.where(at == first + 1, low, 0))


def column(block, lane):
    at = iota((1, LANES), 1)
    weight = jnp.where(at == lane, float(1 << DIGIT), jnp.where(at == lane + 1, 1.0, 0.0))
    return jnp.sum(block * weight, axis=1, keepdims=True).astype(I32)


def order(step, start, count):
    odd = step % 2
    return (start + count // 2 + (1 - odd) * (step // 2) - odd * ((step + 1) // 2) + count) % count


def kernel(
    shards,
    replicas,
    tab_a, tab_b, proj_a, proj_b, owner_a_in, row_a_in, bag_a_in, owner_b_in, row_b_in, bag_b_in, d_pooled_in,
    pooled_out, grads_out, proj_out,
    owner_a, row_a, bag_a, owner_b, row_b, bag_b, d_pooled,
    tabs, proj, slot, give, sent, came, found, back, bags_a, bags_b, grads, looked,
    piece, piece_in, share, share_in, part, part_in, tile, tile_in, done, done_in,
    in_sems, send_sems, came_sems, back_sems, recv_sems,
):
    me, rep = lax.axis_index("shard"), lax.axis_index("rep")
    lookups, rows, bags = owner_a.shape[1], tab_a.shape[1], d_pooled.shape[0]
    wide_a, wide_b = tab_a.shape[0], tab_b.shape[0]
    wide = wide_a + wide_b
    per_group = shards // GROUPS
    slots = per_group * SLOT_ROWS
    my_group = me // per_group
    holders, per = part.shape[0], part.shape[1] // TILE
    stride = shards // holders

    loads = [
        pltpu.make_async_copy(source, target, in_sems.at[k])
        for k, (source, target) in enumerate(
            (
                (owner_a_in, owner_a),
                (owner_b_in, owner_b),
                (bag_a_in, bag_a),
                (bag_b_in, bag_b),
                (row_a_in, row_a),
                (row_b_in, row_b),
                (proj_a, proj.at[0:wide_a]),
                (proj_b, proj.at[wide_a:wide]),
                (d_pooled_in, d_pooled),
                (tab_a, tabs.at[0, 0:wide_a]),
                (tab_b, tabs.at[1, wide_a:wide]),
            )
        )
    ]
    for load in loads:
        load.start()
    barrier = pltpu.get_barrier_semaphore()

    def each_rep(visit):
        def one(step, carry):
            visit(order(step, rep, replicas))
            return carry

        lax.fori_loop(0, replicas - 1, one, 0)

    def each_shard(visit):
        def group_of(step, carry):
            first = order(step, my_group, GROUPS) * per_group

            def one(i, inner):
                visit(first + i)
                return inner

            return lax.fori_loop(0, per_group, one, carry)

        lax.fori_loop(0, GROUPS - 1, group_of, 0)

        def beside(i, carry):
            visit(my_group * per_group + (me + i) % per_group)
            return carry

        lax.fori_loop(1, per_group, beside, 0)

    def greet(*target):
        pl.semaphore_signal(barrier, inc=1, device_id=target, device_id_type=pl.DeviceIdType.MESH)

    each_rep(lambda target: greet(me, target))
    each_shard(lambda target: greet(target, rep))

    proj[wide:, :] = jnp.zeros((LANES - wide, proj.shape[1]), BF16)
    tabs[0, wide_a:, :] = jnp.zeros((LANES - wide_a, rows), BF16)
    tabs[1, 0:wide_a, :] = jnp.zeros((wide_a, rows), BF16)
    tabs[1, wide:, :] = jnp.zeros((LANES - wide, rows), BF16)
    give[0, wide_a:wide, :] = jnp.zeros((wide - wide_a, lookups), BF16)
    give[1, 0:wide_a, :] = jnp.zeros((wide_a, lookups), BF16)
    for load in loads[:9]:
        load.wait()

    row_grad = dot(proj[...], d_pooled[...], ((1,), (1,))).astype(BF16)
    chunk = min(256, lookups)
    before = onehot(iota((chunk, chunk), 0) < iota((chunk, chunk), 1))
    carried = jnp.zeros((2 * shards, 1), F32)
    for first in range(0, lookups, chunk):
        cut = slice(first, first + chunk)
        named_a = owner_a[:, cut] == iota((shards, chunk), 0)
        named_b = owner_b[:, cut] == iota((shards, chunk), 0)
        named = jnp.concatenate([jnp.where(named_a, 1.0, 0.0), jnp.where(named_b, 1.0, 0.0)])
        earlier = dot(named.astype(BF16), before) + carried
        carried = carried + jnp.sum(named, axis=1, keepdims=True)
        earlier = earlier * named
        place_a = jnp.sum(earlier[:shards], axis=0, keepdims=True).astype(I32)
        place_b = jnp.sum(earlier[shards:], axis=0, keepdims=True).astype(I32)
        slot[0:1, cut] = owner_a[:, cut] * SLOT_ROWS + place_a
        slot[1:2, cut] = owner_b[:, cut] * SLOT_ROWS + place_b
        in_bag = onehot(bag_a[:, cut] == iota((bags, chunk), 0))
        give[0, 0:wide_a, cut] = dot(row_grad[0:wide_a], in_bag).astype(BF16)
        in_bag = onehot(bag_b[:, cut] == iota((bags, chunk), 0))
        give[1, wide_a:wide, cut] = dot(row_grad[wide_a:wide], in_bag).astype(BF16)
        tail = (LANES - wide, chunk)
        give[0, wide:, cut] = (digits(row_a[:, cut], 0, tail) + digits(bag_a[:, cut] + 1, 2, tail)).astype(F32).astype(BF16)
        give[1, wide:, cut] = (digits(row_b[:, cut], 4, tail) + digits(bag_b[:, cut] + 1, 6, tail)).astype(F32).astype(BF16)

    def fill(step):
        group = order(step, my_group, GROUPS)
        at = iota((slots, lookups), 0) + group * slots
        block = dot(onehot(slot[0:1, :] == at), give[0], ((1,), (1,)))
        block += dot(onehot(slot[1:2, :] == at), give[1], ((1,), (1,)))
        sent[pl.ds(group * per_group, per_group)] = block.reshape(per_group, SLOT_ROWS, LANES).astype(BF16)

    fill(0)
    pl.semaphore_wait(barrier, shards + replicas - 2)

    def to_shard(block, there, target, send_sem, recv_sem):
        pltpu.make_async_remote_copy(
            src_ref=block,
            dst_ref=there,
            send_sem=send_sem,
            recv_sem=recv_sem,
            device_id=(target, rep),
            device_id_type=pl.DeviceIdType.MESH,
        ).start()

    def to_rep(block, there, target, send_sem, recv_sem):
        pltpu.make_async_remote_copy(
            src_ref=block,
            dst_ref=there,
            send_sem=send_sem,
            recv_sem=recv_sem,
            device_id=(me, target),
            device_id_type=pl.DeviceIdType.MESH,
        ).start()

    def send_group(group, source, landing, send_sem, recv_sem):
        def one(i, carry):
            target = group * per_group + i

            @pl.when(target != me)
            def _():
                to_shard(source.at[target], landing.at[me], target, send_sem, recv_sem)

            @pl.when(target == me)
            def _():
                pltpu.make_async_copy(source.at[target], landing.at[me], recv_sem).start()

            return carry

        lax.fori_loop(0, per_group, one, 0)

    def ask(step, carry):
        send_group(order(step, my_group, GROUPS), sent, came, send_sems.at[0], came_sems.at[my_group])
        fill(step + 1)
        return carry

    lax.fori_loop(0, GROUPS - 1, ask, 0)
    send_group(order(GROUPS - 1, my_group, GROUPS), sent, came, send_sems.at[0], came_sems.at[my_group])

    grads[...] = jnp.zeros_like(grads)
    looked[...] = jnp.zeros_like(looked)

    for load in loads[9:]:
        load.wait()

    def answer(step, carry):
        group = order(step, my_group, GROUPS)
        mine = pl.ds(group * per_group, per_group)
        wait_bytes(came.at[mine], came_sems.at[group])
        block = came[mine].astype(F32).reshape(slots, LANES)
        at = iota((slots, rows), 1)
        hot_a = onehot(column(block, wide) == at)
        hot_b = onehot(column(block, wide + 4) == at)
        gathered = dot(hot_a, tabs[0], ((1,), (1,))) + dot(hot_b, tabs[1], ((1,), (1,)))
        found[mine] = gathered.reshape(per_group, SLOT_ROWS, LANES).astype(BF16)
        send_group(group, found, back, send_sems.at[1], back_sems.at[my_group])
        turned = block.T.astype(BF16)
        grads[0:wide_a, :] += dot(turned[0:wide_a], hot_a)
        grads[wide_a:wide, :] += dot(turned[wide_a:wide], hot_b)
        return carry

    lax.fori_loop(0, GROUPS, answer, 0)

    tall, broad = piece.shape[1], piece.shape[2]
    across = rows // broad
    for k in range(replicas):
        high, left = (k // across) * tall, (k % across) * broad
        piece[k] = grads[high : high + tall, left : left + broad].astype(BF16)
    piece_in[rep] = piece[rep]

    each_rep(lambda target: to_rep(piece.at[target], piece_in.at[rep], target, send_sems.at[2], recv_sems.at[0]))

    def mark(group, carry):
        block = sent[pl.ds(group * per_group, per_group)].astype(F32).reshape(slots, LANES)
        at = iota((slots, bags), 1) + 1
        bags_a[pl.ds(group * slots, slots), :] = onehot(column(block, wide + 2) == at)
        bags_b[pl.ds(group * slots, slots), :] = onehot(column(block, wide + 6) == at)
        return carry

    lax.fori_loop(0, GROUPS, mark, 0)

    def pool(step, carry):
        group = order(step, my_group, GROUPS)
        mine = pl.ds(group * per_group, per_group)
        wait_bytes(back.at[mine], back_sems.at[group])
        turned = back[mine].astype(F32).reshape(slots, LANES).T.astype(BF16)
        here = pl.ds(group * slots, slots)
        looked[0:wide_a, :] += dot(turned[0:wide_a], bags_a[here, :])
        looked[wide_a:wide, :] += dot(turned[wide_a:wide], bags_b[here, :])
        return carry

    lax.fori_loop(0, GROUPS, pool, 0)

    high = looked[...].astype(BF16)
    low = (looked[...] - high.astype(F32)).astype(BF16)
    partial = dot(high, d_pooled[...]) + dot(low, d_pooled[...])
    embed = partial.shape[1]
    halves = embed // LANES
    for k in range(holders * per):
        top, left = (k // halves) * TILE, (k % halves) * LANES
        first = (k % per) * TILE
        part[k // per, first : first + TILE, :] = partial[top : top + TILE, left : left + LANES].astype(BF16)
    index = me // stride
    holding = jnp.logical_and(me == index * stride, index < holders)

    def hand(step, carry):
        target = (index + step) % holders

        @pl.when(target * stride != me)
        def _():
            to_shard(part.at[target], part_in.at[me], target * stride, send_sems.at[4], recv_sems.at[2])

        return carry

    lax.fori_loop(0, holders, hand, 0)

    @pl.when(holding)
    def _():
        part_in[me] = part[index]
        wait_bytes(part_in.at[pl.ds(0, shards - 1)], recv_sems.at[2])
        tile[...] = jnp.sum(part_in[...].astype(F32), axis=0).astype(BF16)
        tile_in[rep] = tile[...]
        each_rep(lambda target: to_rep(tile, tile_in.at[rep], target, send_sems.at[5], recv_sems.at[3]))

    wait_bytes(piece_in.at[pl.ds(0, replicas - 1)], recv_sems.at[0])
    share[...] = jnp.sum(piece_in[...].astype(F32), axis=0).astype(BF16)
    share_in[rep] = share[...]

    each_rep(lambda target: to_rep(share, share_in.at[rep], target, send_sems.at[3], recv_sems.at[1]))

    @pl.when(holding)
    def _():
        wait_bytes(tile_in.at[pl.ds(0, replicas - 1)], recv_sems.at[3])
        scale = 1.0 / (float(lookups * shards * replicas) ** 0.5)
        done[...] = (jnp.sum(tile_in[...].astype(F32), axis=0) * scale).astype(BF16)
        done_in[index] = done[...]
        each_shard(lambda target: to_shard(done, done_in.at[index], target, send_sems.at[6], recv_sems.at[4]))

    turned = looked[...].T
    high = turned.astype(BF16)
    low = (turned - high.astype(F32)).astype(BF16)
    pooled_out[...] = (dot(high, proj[...]) + dot(low, proj[...])).astype(BF16)

    wait_bytes(share_in.at[pl.ds(0, replicas - 1)], recv_sems.at[1])
    for k in range(replicas):
        top, left = (k // across) * tall, (k % across) * broad
        grads_out[top : top + tall, left : left + broad] = share_in[k]

    @pl.when(holding)
    def _():
        wait_bytes(done_in.at[pl.ds(0, holders - 1)], recv_sems.at[4])

    @pl.when(jnp.logical_not(holding))
    def _():
        wait_bytes(done_in, recv_sems.at[4])

    for k in range(holders * per):
        top, left = (k // halves) * TILE, (k % halves) * LANES
        first = (k % per) * TILE
        proj_out[top : top + TILE, left : left + LANES] = done_in[k // per, first : first + TILE, :].astype(F32)

    wait_bytes(sent.at[pl.ds(0, shards - 1)], send_sems.at[0])
    wait_bytes(found.at[pl.ds(0, shards - 1)], send_sems.at[1])
    wait_bytes(piece.at[pl.ds(0, replicas - 1)], send_sems.at[2])
    wait_bytes(share_in.at[pl.ds(0, replicas - 1)], send_sems.at[3])

    @pl.when(holding)
    def _():
        wait_bytes(part.at[pl.ds(0, holders - 1)], send_sems.at[4])
        wait_bytes(tile_in.at[pl.ds(0, replicas - 1)], send_sems.at[5])
        wait_bytes(part_in.at[pl.ds(0, shards - 1)], send_sems.at[6])

    @pl.when(jnp.logical_not(holding))
    def _():
        wait_bytes(part, send_sems.at[4])


def finish(pooled, grads, grad_proj, pooled_out, grad_a, grad_b, proj_a, proj_b):
    wide_a = grad_a.shape[0]
    pooled_out[...] = pooled[...]
    grad_a[...] = grads[0:wide_a, :].astype(F32)
    grad_b[...] = grads[wide_a:, :].astype(F32)
    proj_a[...] = grad_proj[0:wide_a, :]
    proj_b[...] = grad_proj[wide_a:, :]


def body(table_a, table_b, proj_a, proj_b, owner_a, row_a, bag_a, owner_b, row_b, bag_b, d_pooled):
    shards, replicas = lax.axis_size("shard"), lax.axis_size("rep")
    lookups = row_a.shape[0]
    rows, wide_a = table_a.shape
    wide = wide_a + table_b.shape[1]
    bags, embed = d_pooled.shape
    tiles = wide * embed // (TILE * LANES)
    holders = max(h for h in range(1, min(tiles, shards) + 1) if tiles % h == 0)
    per = tiles // holders
    tall, broad = wide // 2, 2 * rows // replicas
    block = pltpu.VMEM((shards, SLOT_ROWS, LANES), BF16)
    line = (1, lookups)
    pooled, grads, grad_proj = pl.pallas_call(
        functools.partial(kernel, shards, replicas),
        out_shape=(
            jax.ShapeDtypeStruct((bags, embed), BF16),
            jax.ShapeDtypeStruct((wide, rows), BF16),
            jax.ShapeDtypeStruct((wide, embed), F32),
        ),
        in_specs=[pl.BlockSpec(memory_space=pltpu.HBM)] * 11,
        out_specs=(pl.BlockSpec(memory_space=pltpu.VMEM),) * 3,
        scratch_shapes=[
            pltpu.VMEM(line, I32),
            pltpu.VMEM(line, I32),
            pltpu.VMEM(line, I32),
            pltpu.VMEM(line, I32),
            pltpu.VMEM(line, I32),
            pltpu.VMEM(line, I32),
            pltpu.VMEM((bags, embed), BF16),
            pltpu.VMEM((2, LANES, rows), BF16),
            pltpu.VMEM((LANES, embed), BF16),
            pltpu.VMEM((8, lookups), I32),
            pltpu.VMEM((2, LANES, lookups), BF16),
            block,
            block,
            block,
            block,
            pltpu.VMEM((shards * SLOT_ROWS, bags), BF16),
            pltpu.VMEM((shards * SLOT_ROWS, bags), BF16),
            pltpu.VMEM((wide, rows), F32),
            pltpu.VMEM((LANES, bags), F32),
            pltpu.VMEM((replicas, tall, broad), BF16),
            pltpu.VMEM((replicas, tall, broad), BF16),
            pltpu.VMEM((tall, broad), BF16),
            pltpu.VMEM((replicas, tall, broad), BF16),
            pltpu.VMEM((holders, TILE * per, LANES), BF16),
            pltpu.VMEM((shards, TILE * per, LANES), BF16),
            pltpu.VMEM((TILE * per, LANES), BF16),
            pltpu.VMEM((replicas, TILE * per, LANES), BF16),
            pltpu.VMEM((TILE * per, LANES), BF16),
            pltpu.VMEM((holders, TILE * per, LANES), BF16),
            pltpu.SemaphoreType.DMA((11,)),
            pltpu.SemaphoreType.DMA((7,)),
            pltpu.SemaphoreType.DMA((GROUPS,)),
            pltpu.SemaphoreType.DMA((GROUPS,)),
            pltpu.SemaphoreType.DMA((5,)),
        ],
        compiler_params=pltpu.CompilerParams(
            collective_id=0, has_side_effects=True, vmem_limit_bytes=LIMIT
        ),
    )(
        *(
            pltpu.with_memory_space_constraint(x, pltpu.HBM)
            for x in (
                table_a.T,
                table_b.T,
                proj_a,
                proj_b,
                owner_a.reshape(line),
                row_a.reshape(line),
                bag_a,
                owner_b.reshape(line),
                row_b.reshape(line),
                bag_b,
                d_pooled,
            )
        )
    )
    pooled, grad_a, grad_b, proj_grad_a, proj_grad_b = pl.pallas_call(
        finish,
        out_shape=(
            jax.ShapeDtypeStruct((bags, embed), BF16),
            jax.ShapeDtypeStruct((wide_a, rows), F32),
            jax.ShapeDtypeStruct((wide - wide_a, rows), F32),
            jax.ShapeDtypeStruct((wide_a, embed), F32),
            jax.ShapeDtypeStruct((wide - wide_a, embed), F32),
        ),
        in_specs=[pl.BlockSpec(memory_space=pltpu.VMEM)] * 3,
        out_specs=(pl.BlockSpec(memory_space=pltpu.VMEM),) * 5,
        compiler_params=pltpu.CompilerParams(vmem_limit_bytes=SMALL),
    )(pooled, grads, grad_proj)
    return (pooled, grad_a.T, grad_b.T, proj_grad_a, proj_grad_b)


def solution(mesh):
    split = ("shard", "rep")
    tier = (P(split, None), P(split), P(split, None))
    in_specs = (P("shard", None), P("shard", None), P(), P(), *tier, *tier, P(split, None))
    out_specs = (P(split, None), P("shard", None), P("shard", None), P(), P())
    return jax.shard_map(body, mesh=mesh, in_specs=in_specs, out_specs=out_specs, check_vma=False)
```
